512 devices in a mesh: dom: 64 (over y, z), edge: 8 (over x, core).
Axes of the slice: x: 4, y: 4, z: 16, core: 2. Of those that a mesh axis runs over, the one named last changes fastest.
Arguments:
- node_rows: bfloat16 [16384, 512], P('dom'), may hold values from -6 to 6
- w_first: bfloat16 [1536, 512], replicated, may hold values from -0.15625 to 0.15625
- w_second: bfloat16 [512, 128], replicated, may hold values from -0.25 to 0.25
- w_third: bfloat16 [128], replicated, may hold values from -1 to 1
- src_row: int32 [524288], P(('dom', 'edge')), may hold values from 0 to 255, as said below
- requests: int32 [32768, 8], P(('dom', 'edge')), may hold values from 0 to 255
- slot_index: int32 [524288], P(('dom', 'edge')), may hold values from 0 to 511
- labels: int32 [524288], P(('dom', 'edge')), may hold values from 0 to 1
- live_count: int32 [512], P(('dom', 'edge')), may hold values from 204 to 1024, as said below
Outputs:
- grad_first: float32 [1536, 512], P('edge', 'dom')
- grad_second: float32 [512, 128], P('dom', 'edge')
- grad_third: float32 [128], replicated
- pair_loss: float32 [], replicated
- node_grad: float32 [16384, 512], P(('dom', 'edge'))
The draws below stay inside these ranges and needn't reach their ends.
Inputs may be any that keep to these rules, and one draw needn't show every extreme that they name: `src_row`: each device's 1024 entries are sorted, non-decreasing. `live_count`: some device is full in every draw.
All inputs are finite; a program needn't handle non-finite values.
Results may differ from the reference program's by a relative error of at most 0.0048.
Values may be sent and summed in bfloat16 or wider, within the bound.
No kernel may reach another device: no remote copies, remote signals or barrier semaphores. Data moves between devices by JAX's collectives and lax.ppermute only.
A program may use at most 64 MiB of HBM per device.

```python
import math
import jax
import jax.numpy as jnp
from jax import lax

D = 512
H1 = 512
H2 = 128
NODE_DEV = 256
E_DEV = 1024
CAP = 8
NODES = 16384
EDGES = 524288
N_DOM = 64
N_EDGE = 8


def draw_src_row(key, part):
    key = jax.random.fold_in(key, 11)
    n_dev = N_DOM * N_EDGE
    drawn = jax.random.randint(key, (n_dev, E_DEV), 0, NODE_DEV, dtype=jnp.int32)
    drawn = drawn.at[:, 0].set(0).at[:, 1].set(NODE_DEV - 1)
    return jnp.sort(drawn, axis=1).reshape(n_dev * E_DEV)


def draw_requests(key, part):
    key = jax.random.fold_in(key, 23)
    drawn = jax.random.randint(key, (N_DOM * N_EDGE * N_DOM, CAP), 0, NODE_DEV, dtype=jnp.int32)
    return drawn.at[0, 0].set(NODE_DEV - 1)


def draw_slot_index(key, part):
    key = jax.random.fold_in(key, 37)
    n_dev = N_DOM * N_EDGE
    drawn = jax.random.randint(key, (n_dev, E_DEV), 0, N_DOM * CAP, dtype=jnp.int32)
    drawn = drawn.at[:, 0].set(N_DOM * CAP - 1).at[:, 1].set(0)
    return drawn.reshape(n_dev * E_DEV)


def draw_live_count(key, part):
    key = jax.random.fold_in(key, 41)
    n_dev = N_DOM * N_EDGE
    key_hub, key_light, key_full, key_least = jax.random.split(key, 4)
    is_hub = jax.random.randint(key_hub, (n_dev,), 0, 8, dtype=jnp.int32) == 0
    light = jax.random.randint(key_light, (n_dev,), E_DEV // 5, E_DEV // 3 + 1, dtype=jnp.int32)
    counts = jnp.where(is_hub, E_DEV, light).astype(jnp.int32)
    full_at = jax.random.randint(key_full, (), 0, n_dev, dtype=jnp.int32)
    least_at = (full_at + 1 + jax.random.randint(key_least, (), 0, n_dev - 1, dtype=jnp.int32)) % n_dev
    return counts.at[full_at].set(E_DEV).at[least_at].set(E_DEV // 5)


def plant(entries, stream_key, low, high):
    extent = entries.shape
    place = [jax.random.randint(jax.random.fold_in(stream_key, axis), (), 0, extent[axis]) for axis in range(len(extent))]
    entries = entries.at[tuple(place)].set(low)
    longest = extent.index(max(extent))
    place[longest] = (place[longest] + 1) % extent[longest]
    return entries.at[tuple(place)].set(high)


def levels(stream_key, shape, pieces, smallest, high):
    gain = 1.0
    for dim, shards_of in pieces:
        steps = jax.random.uniform(jax.random.fold_in(jax.random.fold_in(stream_key, 6), dim), (shards_of,), jnp.float32, smallest / len(pieces), high / len(pieces))
        gain = gain * jnp.repeat(jnp.exp(steps), shape[dim] // shards_of).reshape((-1,) + (1,) * (len(shape) - 1 - dim))
    return gain


def bell_draw(rng, dims, scale, bound, pieces=(), held_as=jnp.bfloat16):
    values = jax.random.normal(rng, dims, jnp.float32) * scale
    if len(pieces) > 0:
        values = levels(rng, dims, pieces, -0.22, 0.18) * values
    return jnp.clip(values, min=-bound, max=bound).astype(held_as)


def setup_inputs(seed: int = 0) -> dict:
    keys = jax.random.split(jax.random.key(seed), 10)
    return {
        "node_rows": bell_draw(keys[0], (NODES, D), 1.0, 6.0, ((0, 64),)),
        "w_first": bell_draw(keys[1], (3 * D, H1), (3 * D) ** -0.5, 0.15625),
        "w_second": bell_draw(keys[2], (H1, H2), H1 ** -0.5, 0.25),
        "w_third": bell_draw(keys[3], (H2,), (H2 // 4) ** -0.5, 1.0),
        "src_row": draw_src_row(jax.random.fold_in(keys[9], 71), 0),
        "requests": draw_requests(jax.random.fold_in(keys[9], 71), 0),
        "slot_index": draw_slot_index(jax.random.fold_in(keys[9], 71), 0),
        "labels": plant(jax.random.randint(keys[7], (EDGES,), 0, 2), jax.random.fold_in(keys[7], 1), 0, 1).astype(jnp.int32),
        "live_count": draw_live_count(jax.random.fold_in(keys[9], 71), 0),
    }


def dsilu(values):
    sig = jax.nn.sigmoid(values)
    return sig * (1.0 + values * (1.0 - sig))

def first_dim(left, right):
    return lax.dot_general(left, right, (((0,), (0,)), ((), ())), preferred_element_type=jnp.float32)

def last_dim(left, right):
    return lax.dot_general(left, right, (((1,), (1,)), ((), ())), preferred_element_type=jnp.float32)

def pair_pass(near_rows, far_rows, w_first, w_second, w_third, labels, is_live, loss_scale, width):
    product = (near_rows.astype(jnp.float32) * far_rows.astype(jnp.float32)).astype(jnp.bfloat16)
    features = jnp.concatenate([near_rows, far_rows, product], axis=1)
    pre_first = jnp.dot(features, w_first, preferred_element_type=jnp.float32)
    first = jax.nn.silu(pre_first).astype(jnp.bfloat16)
    pre_second = jnp.dot(first, w_second, preferred_element_type=jnp.float32)
    second = jax.nn.silu(pre_second).astype(jnp.bfloat16)
    logits = jnp.dot(second, w_third, preferred_element_type=jnp.float32)
    target = labels.astype(jnp.float32)
    slope = is_live * (jax.nn.sigmoid(logits) - target)
    pair_loss = loss_scale * jnp.sum(is_live * (jax.nn.softplus(logits) - target * logits))
    grad_third = loss_scale * jnp.dot(slope, second.astype(jnp.float32), precision=lax.Precision.HIGHEST)
    back_second = (slope[:, None] * w_third.astype(jnp.float32)[None, :] * dsilu(pre_second)).astype(jnp.bfloat16)
    grad_second = loss_scale * first_dim(first, back_second)
    back_first = (last_dim(back_second, w_second) * dsilu(pre_first)).astype(jnp.bfloat16)
    grad_first = loss_scale * first_dim(features, back_first)
    feature_grad = last_dim(back_first, w_first)
    block_a = feature_grad[:, :width]
    block_b = feature_grad[:, width:2 * width]
    block_c = feature_grad[:, 2 * width:]
    near_grad = block_a + block_c * far_rows.astype(jnp.float32)
    far_grad = block_b + block_c * near_rows.astype(jnp.float32)
    return (grad_first, grad_second, grad_third, pair_loss, near_grad, far_grad)

def reference(node_rows, w_first, w_second, w_third, src_row, requests, slot_index, labels, live_count):
    n_dev = N_DOM * N_EDGE
    width = node_rows.shape[1]
    loss_scale = 1.0 / math.sqrt(E_DEV * n_dev)
    src_all = src_row.reshape(n_dev, E_DEV)
    slot_all = slot_index.reshape(n_dev, E_DEV)
    label_all = labels.reshape(n_dev, E_DEV)
    asked_all = requests.reshape(n_dev, N_DOM * CAP)
    device_ids = jnp.arange(n_dev, dtype=jnp.int32)

    def visit(totals, inputs):
        src_here, slot_here, label_here, asked_here, count_here, device_id = inputs
        part_id = device_id // N_EDGE
        near_node = (part_id * NODE_DEV + src_here).astype(jnp.int32)
        far_node = (slot_here // CAP * NODE_DEV + jnp.take(asked_here, slot_here)).astype(jnp.int32)
        near_rows = jnp.take(node_rows, near_node, axis=0)
        far_rows = jnp.take(node_rows, far_node, axis=0)
        is_live = (jnp.arange(E_DEV, dtype=jnp.int32) < count_here).astype(jnp.float32)
        g_first, g_second, g_third, loss_part, near_grad, far_grad = pair_pass(near_rows, far_rows, w_first, w_second, w_third, label_here, is_live, loss_scale, width)
        node_total = totals[4].at[near_node].add(near_grad).at[far_node].add(far_grad)
        return ((totals[0] + g_first, totals[1] + g_second, totals[2] + g_third, totals[3] + loss_part, node_total), None)
    start = (jnp.zeros((3 * D, H1), jnp.float32), jnp.zeros((H1, H2), jnp.float32), jnp.zeros((H2,), jnp.float32), jnp.zeros((), jnp.float32), jnp.zeros((NODE_DEV * N_DOM, D), jnp.float32))
    totals, unused = lax.scan(visit, start, (src_all, slot_all, label_all, asked_all, live_count, device_ids))
    return (totals[0], totals[1], totals[2], totals[3], totals[4])
```

```python
import math

import jax
import jax.numpy as jnp
from jax import lax
from jax.sharding import PartitionSpec as P

BF = jnp.bfloat16
F32 = jnp.float32


def dsilu(values):
    sig = jax.nn.sigmoid(values)
    return sig * (1.0 + values * (1.0 - sig))


def first_dim(left, right):
    return lax.dot_general(left, right, (((0,), (0,)), ((), ())), preferred_element_type=F32)


def last_dim(left, right):
    return lax.dot_general(left, right, (((1,), (1,)), ((), ())), preferred_element_type=F32)


def halves(values):
    high = lax.reduce_precision(values, 8, 7)
    return high.astype(BF), (values - high).astype(BF)


def onehot_rows(index, count):
    return (jnp.arange(count, dtype=jnp.int32)[:, None] == index[None, :]).astype(BF)


def collect(values, index, count):
    onehot = onehot_rows(index, count)
    high, low = halves(values)
    return jnp.dot(onehot, high, preferred_element_type=F32) + jnp.dot(
        onehot, low, preferred_element_type=F32
    )


def pair_pass(near_rows, far_rows, w_first, w_second, w_third, labels, is_live, loss_scale, width):
    product = (near_rows.astype(F32) * far_rows.astype(F32)).astype(BF)
    features = jnp.concatenate([near_rows, far_rows, product], axis=1)
    pre_first = jnp.dot(features, w_first, preferred_element_type=F32)
    first = jax.nn.silu(pre_first).astype(BF)
    pre_second = jnp.dot(first, w_second, preferred_element_type=F32)
    second = jax.nn.silu(pre_second).astype(BF)
    logits = jnp.dot(second, w_third, preferred_element_type=F32)
    target = labels.astype(F32)
    slope = is_live * (jax.nn.sigmoid(logits) - target)
    pair_loss = loss_scale * jnp.sum(is_live * (jax.nn.softplus(logits) - target * logits))
    grad_third = loss_scale * jnp.dot(slope, second.astype(F32), precision=lax.Precision.HIGHEST)
    back_second = (slope[:, None] * w_third.astype(F32)[None, :] * dsilu(pre_second)).astype(BF)
    grad_second_t = loss_scale * first_dim(back_second, first)
    back_first = (last_dim(back_second, w_second) * dsilu(pre_first)).astype(BF)
    grad_first = loss_scale * first_dim(features, back_first)
    feature_grad = last_dim(back_first, w_first)
    block_a = feature_grad[:, :width]
    block_b = feature_grad[:, width : 2 * width]
    block_c = feature_grad[:, 2 * width :]
    near_grad = block_a + block_c * far_rows.astype(F32)
    far_grad = block_b + block_c * near_rows.astype(F32)
    return (grad_first, grad_second_t, grad_third, pair_loss, near_grad, far_grad)


def body(node_rows, w_first, w_second, w_third, src_row, requests, slot_index, labels, live_count):
    own_count, width = node_rows.shape
    per_device = src_row.shape[0]
    parts, cap = requests.shape
    n_edge = lax.axis_size("edge")
    chips = n_edge // 2
    slots = parts * cap
    hidden = w_first.shape[1]
    hidden2 = w_second.shape[1]
    loss_scale = 1.0 / math.sqrt(per_device * parts * n_edge)
    edge = lax.axis_index("edge")
    chip, core = edge // 2, edge % 2
    sibling = [(i, i ^ 1) for i in range(n_edge)]

    def ahead(step):
        return [(i, (i + 2 * step) % n_edge) for i in range(n_edge)]

    steps = (1, chips - 1) + tuple(range(2, chips - 1))

    def by_core(blocks):
        rolled = jnp.roll(blocks, -2 * chip, axis=0)
        rolled = rolled.reshape((chips, 2) + blocks.shape[1:])
        kept = lax.dynamic_index_in_dim(rolled, core, 1, keepdims=False)
        sent = lax.dynamic_index_in_dim(rolled, 1 - core, 1, keepdims=False)
        return kept + lax.ppermute(sent, "edge", sibling)

    asked_here = lax.all_to_all(requests, "dom", split_axis=0, concat_axis=0, tiled=True)
    asked_flat = asked_here.reshape(slots)
    answer = jnp.take(node_rows, asked_flat, axis=0, mode="clip").reshape(parts, cap, width)
    replies = lax.all_to_all(answer, "dom", split_axis=0, concat_axis=0, tiled=True)
    far_rows = jnp.take(replies.reshape(slots, width), slot_index, axis=0, mode="clip")
    near_rows = jnp.take(node_rows, src_row, axis=0, mode="clip")
    is_live = (jnp.arange(per_device, dtype=jnp.int32) < live_count[0]).astype(F32)
    g_first, g_second_t, g_third, loss_part, near_grad, far_grad = pair_pass(
        near_rows, far_rows, w_first, w_second, w_third, labels, is_live, loss_scale, width
    )

    slot_grad = collect(far_grad, slot_index, slots).astype(BF).reshape(parts, cap, width)
    returned = lax.all_to_all(slot_grad, "dom", split_axis=0, concat_axis=0, tiled=True)

    rows1 = g_first.shape[0] // n_edge
    rows2 = hidden2 // n_edge
    extra = jnp.zeros((8, hidden), F32).at[0, :hidden2].set(g_third).at[1, 0].set(loss_part)
    blocks = jnp.concatenate(
        [
            g_first.reshape(n_edge, rows1, hidden),
            g_second_t.reshape(n_edge, rows2, hidden),
            jnp.broadcast_to(extra, (n_edge, 8, hidden)),
        ],
        axis=1,
    )
    chip_sum = by_core(blocks)
    total = chip_sum[0]
    rows = rows1 + rows2
    for step in steps:
        high, low = halves(chip_sum[step])
        packed = jnp.concatenate([high, low[rows:]], axis=0)
        got = lax.ppermute(packed, "edge", ahead(step)).astype(F32)
        total = total + jnp.concatenate([got[:rows], got[rows : rows + 8] + got[rows + 8 :]], axis=0)

    share = hidden // parts
    small = jnp.concatenate([total[rows, :hidden2], total[rows + 1, :share]]).reshape(-1, share).T
    small_high, small_low = halves(small)
    n_small = small.shape[1]
    columns = total[:rows].T.reshape(parts, share, rows).astype(BF)
    sent = jnp.concatenate(
        [
            columns,
            jnp.broadcast_to(small_high, (parts, share, n_small)),
            jnp.broadcast_to(small_low, (parts, share, n_small)),
        ],
        axis=2,
    )
    got = lax.all_to_all(sent, "dom", split_axis=0, concat_axis=0, tiled=True)
    got = jnp.sum(got.astype(F32), axis=0)
    first_share = got[:, :rows1].T
    second_share = got[:, rows1:rows]
    small = got[:, rows : rows + n_small] + got[:, rows + n_small :]
    small = small.T.reshape(-1)
    third_total = small[:hidden2]
    loss_total = small[hidden2]

    owned = collect(near_grad, src_row, own_count)
    owned = owned + jnp.dot(
        onehot_rows(asked_flat, own_count),
        returned.reshape(slots, width),
        preferred_element_type=F32,
    )
    node_chip = by_core(owned.reshape(n_edge, own_count // n_edge, width))
    node_share = node_chip[0]
    for step in steps:
        node_share = node_share + lax.ppermute(node_chip[step], "edge", ahead(step))
    return (first_share, second_share, third_total, loss_total, node_share)


def solution(mesh):
    in_specs = (
        P("dom", None),
        P(),
        P(),
        P(),
        P(("dom", "edge")),
        P(("dom", "edge"), None),
        P(("dom", "edge")),
        P(("dom", "edge")),
        P(("dom", "edge")),
    )
    out_specs = (P("edge", "dom"), P("dom", "edge"), P(), P(), P(("dom", "edge"), None))
    return jax.shard_map(body, mesh=mesh, in_specs=in_specs, out_specs=out_specs, check_vma=False)
```

```python
import functools
import math

import jax
import jax.numpy as jnp
from jax import lax
from jax.experimental import pallas as pl
from jax.experimental.pallas import tpu as pltpu
from jax.sharding import PartitionSpec as P

BF = jnp.bfloat16
F32 = jnp.float32
I32 = jnp.int32
MIB = 1 << 20
TILE = 512
WHOLE = pl.BlockSpec(memory_space=pltpu.VMEM)
SCALARS = pl.BlockSpec(memory_space=pltpu.SMEM)


def dot(left, right, left_dim=1, right_dim=0):
    return lax.dot_general(
        left, right, (((left_dim,), (right_dim,)), ((), ())), preferred_element_type=F32
    )


def halves(values):
    high = values.astype(BF)
    return high, (values - high.astype(F32)).astype(BF)


def onehot(index, shape, axis):
    return jnp.where(index == lax.broadcasted_iota(I32, shape, axis), 1.0, 0.0).astype(BF)


def params(mib):
    return pltpu.CompilerParams(vmem_limit_bytes=mib * MIB)


def cost(flops, nbytes):
    return pl.CostEstimate(flops=flops, bytes_accessed=nbytes, transcendentals=0)


def answer_kernel(asked_ref, node_ref, out_ref):
    own_count, slots = node_ref.shape[0], asked_ref.shape[1]
    pick = onehot(asked_ref[...], (own_count, slots), 0)
    out_ref[...] = dot(pick, node_ref[...], 0, 0).astype(BF)


def pair_kernel(
    scale, live_ref, cols_ref, slots_ref, node_ref, rep_ref, wf_ref, ws_ref, wt_ref,
    slot_out, first_out, bfirst_out, bsecond_out, extra_out, acc,
):
    step = pl.program_id(0)
    tile = cols_ref.shape[0]
    own_count, width = node_ref.shape
    slots = rep_ref.shape[0]
    hidden2 = ws_ref.shape[1]

    @pl.when(step == 0)
    def _():
        acc[...] = jnp.zeros_like(acc)
        extra_out[...] = jnp.zeros_like(extra_out)

    near = dot(onehot(cols_ref[:, 0:1], (tile, own_count), 1), node_ref[...])
    far = dot(onehot(cols_ref[:, 1:2], (tile, slots), 1), rep_ref[...])
    target = cols_ref[:, 2:3].astype(F32)
    product = (near * far).astype(BF)
    near_b = near.astype(BF)
    pre_first = (
        dot(near_b, wf_ref[:width])
        + dot(far.astype(BF), wf_ref[width : 2 * width])
        + dot(product, wf_ref[2 * width :])
    )
    sig = jax.nn.sigmoid(pre_first)
    first = (pre_first * sig).astype(BF)
    slope_first = sig * (1.0 + pre_first * (1.0 - sig))
    first_out[...] = first
    pre_second = dot(first, ws_ref[...])
    sig = jax.nn.sigmoid(pre_second)
    second = (pre_second * sig).astype(BF).astype(F32)
    slope_second = sig * (1.0 + pre_second * (1.0 - sig))
    w_third = wt_ref[...].astype(F32)
    logits = jnp.sum(second * w_third, axis=1, keepdims=True)
    place = step * tile + lax.broadcasted_iota(I32, (tile, 1), 0)
    live = jnp.where(place < live_ref[0], 1.0, 0.0)
    slope = live * (jax.nn.sigmoid(logits) - target)
    softplus = jnp.maximum(logits, 0.0) + jnp.log1p(jnp.exp(-jnp.abs(logits)))
    loss = jnp.sum(live * (softplus - target * logits), axis=0, keepdims=True)
    extra_out[0:1, :hidden2] += scale * jnp.sum(slope * second, axis=0, keepdims=True)
    extra_out[1:2, :hidden2] += jnp.broadcast_to(scale * loss, (1, hidden2))
    back_second = (slope * w_third * slope_second).astype(BF)
    bsecond_out[...] = back_second
    back_first = (dot(back_second, ws_ref[...], 1, 1) * slope_first).astype(BF)
    bfirst_out[...] = back_first
    block_b = dot(back_first, wf_ref[width : 2 * width], 1, 1)
    block_c = dot(back_first, wf_ref[2 * width :], 1, 1)
    high, low = halves(block_b + block_c * near)
    place = onehot(slots_ref[...], (slots, tile), 0)
    acc[...] += dot(place, high) + dot(place, low)

    @pl.when(step == pl.num_programs(0) - 1)
    def _():
        slot_out[...] = acc[...].astype(BF)


def weight_kernel(
    scale, n_edge, edge_ref, lines_ref, node_ref, rep_ref, first_ref, bfirst_ref, bsecond_ref, extra_ref,
    kept_out, sent_out, grads, grads2,
):
    own_count, width = node_ref.shape
    slots = rep_ref.shape[0]
    edges = lines_ref.shape[1]
    chips = n_edge // 2
    rows1 = 3 * width // n_edge
    rows2 = grads2.shape[0] // n_edge
    bfirst = bfirst_ref[...]
    near = dot(node_ref[...], onehot(lines_ref[0:1, :], (own_count, edges), 0), 0, 0)
    grads[:width] = scale * dot(near.astype(BF), bfirst)
    far = dot(rep_ref[...], onehot(lines_ref[1:2, :], (slots, edges), 0), 0, 0)
    grads[width : 2 * width] = scale * dot(far.astype(BF), bfirst)
    grads[2 * width :] = scale * dot((near * far).astype(BF), bfirst)
    grads2[...] = scale * dot(bsecond_ref[...], first_ref[...], 0, 0)
    edge = edge_ref[0]
    chip = edge // 2
    core = edge % 2
    for j in range(chips):
        there = 2 * ((chip + j) % chips)
        for out, owner in ((kept_out, there + core), (sent_out, there + 1 - core)):
            out[j, :rows1] = grads[pl.ds(pl.multiple_of(owner * rows1, 8), rows1), :]
            out[j, rows1 : rows1 + rows2] = grads2[pl.ds(pl.multiple_of(owner * rows2, 8), rows2), :]
            out[j, rows1 + rows2 :] = extra_ref[...]


def near_kernel(lines_ref, cols_ref, rep_ref, bfirst_ref, wf_ref, out_ref):
    edges = lines_ref.shape[1]
    slots, width = rep_ref.shape
    bfirst = bfirst_ref[...]
    far = dot(onehot(cols_ref[:, 1:2], (edges, slots), 1), rep_ref[...])
    block_a = dot(bfirst, wf_ref[:width], 1, 1)
    block_c = dot(bfirst, wf_ref[2 * width :], 1, 1)
    high, low = halves(block_a + block_c * far)
    place = onehot(lines_ref[0:1, :], (out_ref.shape[0], edges), 0)
    out_ref[...] = dot(place, high) + dot(place, low)


def owned_kernel(n_edge, edge_ref, asked_ref, near_ref, back_ref, kept_out, sent_out, total):
    own_count = near_ref.shape[0]
    chips = n_edge // 2
    rows = own_count // n_edge
    place = onehot(asked_ref[...], (own_count, asked_ref.shape[1]), 0)
    total[...] = near_ref[...] + dot(place, back_ref[...])
    edge = edge_ref[0]
    chip = edge // 2
    core = edge % 2
    for j in range(chips):
        there = 2 * ((chip + j) % chips)
        for out, owner in ((kept_out, there + core), (sent_out, there + 1 - core)):
            out[j] = total[pl.ds(pl.multiple_of(owner * rows, 8), rows), :]


def body(node_rows, w_first, w_second, w_third, src_row, requests, slot_index, labels, live_count):
    own_count, width = node_rows.shape
    edges = src_row.shape[0]
    parts, cap = requests.shape
    n_edge = lax.axis_size("edge")
    chips = n_edge // 2
    slots = parts * cap
    hidden, hidden2 = w_second.shape
    scale = 1.0 / math.sqrt(edges * parts * n_edge)
    edge = lax.axis_index("edge").astype(I32).reshape(1)
    sibling = [(i, i ^ 1) for i in range(n_edge)]

    def ahead(step):
        return [(i, (i + 2 * step) % n_edge) for i in range(n_edge)]

    steps = (1, chips - 1) + tuple(range(2, chips - 1))
    rows1 = 3 * width // n_edge
    rows2 = hidden2 // n_edge
    rows = rows1 + rows2
    cols = jnp.stack([src_row, slot_index, labels], axis=1)
    lines = jnp.stack([src_row, slot_index], axis=0)

    asked_here = lax.all_to_all(requests, "dom", split_axis=0, concat_axis=0, tiled=True)
    asked_line = asked_here.reshape(1, slots)
    answer = pl.pallas_call(
        answer_kernel,
        out_shape=jax.ShapeDtypeStruct((slots, width), BF),
        in_specs=[WHOLE, WHOLE],
        out_specs=WHOLE,
        compiler_params=params(8),
        name="answer",
    )(asked_line, node_rows)
    replies = lax.all_to_all(
        answer.reshape(parts, cap, width), "dom", split_axis=0, concat_axis=0, tiled=True
    ).reshape(slots, width)

    def fixed(shape):
        return pl.BlockSpec(shape, lambda i: (0,) * len(shape), pipeline_mode=pl.Buffered(1))

    def tiles(count):
        return pl.BlockSpec((TILE, count), lambda i: (i, 0))

    slot_grad, first, back_first, back_second, extra = pl.pallas_call(
        functools.partial(pair_kernel, scale),
        grid=(edges // TILE,),
        out_shape=(
            jax.ShapeDtypeStruct((slots, width), BF),
            jax.ShapeDtypeStruct((edges, hidden), BF),
            jax.ShapeDtypeStruct((edges, hidden), BF),
            jax.ShapeDtypeStruct((edges, hidden2), BF),
            jax.ShapeDtypeStruct((8, hidden), F32),
        ),
        in_specs=[
            SCALARS,
            tiles(3),
            pl.BlockSpec((1, TILE), lambda i: (0, i)),
            fixed((own_count, width)),
            fixed((slots, width)),
            fixed((3 * width, hidden)),
            fixed((hidden, hidden2)),
            fixed((1, hidden2)),
        ],
        out_specs=(
            pl.BlockSpec((slots, width), lambda i: (0, 0)),
            tiles(hidden),
            tiles(hidden),
            tiles(hidden2),
            pl.BlockSpec((8, hidden), lambda i: (0, 0)),
        ),
        scratch_shapes=[pltpu.VMEM((slots, width), F32)],
        compiler_params=params(32),
        cost_estimate=cost(6 * 10**9, 8 * MIB),
        name="pair",
    )(
        live_count, cols, slot_index.reshape(1, edges), node_rows, replies, w_first, w_second,
        w_third.reshape(1, hidden2),
    )

    returned = lax.all_to_all(
        slot_grad.reshape(parts, cap, width), "dom", split_axis=0, concat_axis=0, tiled=True
    ).reshape(slots, width)

    block = jax.ShapeDtypeStruct((chips, rows + 8, hidden), F32)
    kept, sent = pl.pallas_call(
        functools.partial(weight_kernel, scale, n_edge),
        out_shape=(block, block),
        in_specs=[SCALARS] + [WHOLE] * 7,
        out_specs=(WHOLE, WHOLE),
        scratch_shapes=[pltpu.VMEM((3 * width, hidden), F32), pltpu.VMEM((hidden2, hidden), F32)],
        compiler_params=params(32),
        cost_estimate=cost(3 * 10**9, 8 * MIB),
        name="weights",
    )(edge, lines, node_rows, replies, first, back_first, back_second, extra)
    chip_sum = kept + lax.ppermute(sent, "edge", sibling)
    total = chip_sum[0]
    for step in steps:
        high = lax.reduce_precision(chip_sum[step], 8, 7)
        low = chip_sum[step][rows:] - high[rows:]
        packed = jnp.concatenate([high.astype(BF), low.astype(BF)], axis=0)
        got = lax.ppermute(packed, "edge", ahead(step)).astype(F32)
        total = total + jnp.concatenate([got[:rows], got[rows : rows + 8] + got[rows + 8 :]], axis=0)

    share = hidden // parts
    small = jnp.concatenate([total[rows, :hidden2], total[rows + 1, :share]]).reshape(-1, share).T
    small_high = lax.reduce_precision(small, 8, 7)
    small_low = (small - small_high).astype(BF)
    n_small = small.shape[1]
    columns = total[:rows].T.reshape(parts, share, rows).astype(BF)
    packed = jnp.concatenate(
        [
            columns,
            jnp.broadcast_to(small_high.astype(BF), (parts, share, n_small)),
            jnp.broadcast_to(small_low, (parts, share, n_small)),
        ],
        axis=2,
    )
    got = lax.all_to_all(packed, "dom", split_axis=0, concat_axis=0, tiled=True)
    got = jnp.sum(got.astype(F32), axis=0)
    first_share = got[:, :rows1].T
    second_share = got[:, rows1:rows]
    small = got[:, rows : rows + n_small] + got[:, rows + n_small :]
    small = small.T.reshape(-1)
    third_total = small[:hidden2]
    loss_total = small[hidden2]

    near_part = pl.pallas_call(
        near_kernel,
        out_shape=jax.ShapeDtypeStruct((own_count, width), F32),
        in_specs=[WHOLE] * 5,
        out_specs=WHOLE,
        compiler_params=params(32),
        cost_estimate=cost(3 * 10**9, 4 * MIB),
        name="near",
    )(lines, cols, replies, back_first, w_first)
    block = jax.ShapeDtypeStruct((chips, own_count // n_edge, width), F32)
    kept, sent = pl.pallas_call(
        functools.partial(owned_kernel, n_edge),
        out_shape=(block, block),
        in_specs=[SCALARS] + [WHOLE] * 3,
        out_specs=(WHOLE, WHOLE),
        scratch_shapes=[pltpu.VMEM((own_count, width), F32)],
        compiler_params=params(8),
        name="owned",
    )(edge, asked_line, near_part, returned)
    node_chip = kept + lax.ppermute(sent, "edge", sibling)
    node_share = node_chip[0]
    for step in steps:
        node_share = node_share + lax.ppermute(node_chip[step], "edge", ahead(step))
    return (first_share, second_share, third_total, loss_total, node_share)


def solution(mesh):
    in_specs = (
        P("dom", None),
        P(),
        P(),
        P(),
        P(("dom", "edge")),
        P(("dom", "edge"), None),
        P(("dom", "edge")),
        P(("dom", "edge")),
        P(("dom", "edge")),
    )
    out_specs = (P("edge", "dom"), P("dom", "edge"), P(), P(), P(("dom", "edge"), None))
    return jax.shard_map(body, mesh=mesh, in_specs=in_specs, out_specs=out_specs, check_vma=False)
```

```python
import functools
import math

import jax
import jax.numpy as jnp
from jax import lax
from jax.experimental import pallas as pl
from jax.experimental.pallas import tpu as pltpu
from jax.sharding import PartitionSpec as P

BF = jnp.bfloat16
F32 = jnp.float32
I32 = jnp.int32
MIB = 1 << 20
TILE = 512
WHOLE = pl.BlockSpec(memory_space=pltpu.VMEM)
FREE = pl.CostEstimate(flops=0, bytes_accessed=0, transcendentals=0)
SCALARS = pl.BlockSpec(memory_space=pltpu.SMEM)


def dot(left, right, left_dim=1, right_dim=0):
    return lax.dot_general(
        left, right, (((left_dim,), (right_dim,)), ((), ())), preferred_element_type=F32
    )


def halves(values):
    high = values.astype(BF)
    return high, (values - high.astype(F32)).astype(BF)


def onehot(index, shape, axis):
    return jnp.where(index == lax.broadcasted_iota(I32, shape, axis), 1.0, 0.0).astype(BF)


def params(mib):
    return pltpu.CompilerParams(vmem_limit_bytes=mib * MIB)


def cost(flops, nbytes):
    return pl.CostEstimate(flops=flops, bytes_accessed=nbytes, transcendentals=0)


def answer_kernel(asked_ref, node_ref, out_ref):
    own_count, slots = node_ref.shape[0], asked_ref.shape[1]
    pick = onehot(asked_ref[...], (own_count, slots), 0)
    out_ref[...] = dot(pick, node_ref[...], 0, 0).astype(BF)


def pair_kernel(
    scale, live_ref, cols_ref, slots_ref, node_ref, rep_ref, wf_ref, ws_ref, wt_ref,
    slot_out, first_out, bfirst_out, bsecond_out, extra_out, acc,
):
    step = pl.program_id(0)
    tile = cols_ref.shape[0]
    own_count, width = node_ref.shape
    slots = rep_ref.shape[0]
    hidden2 = ws_ref.shape[1]

    @pl.when(step == 0)
    def _():
        acc[...] = jnp.zeros_like(acc)
        extra_out[...] = jnp.zeros_like(extra_out)

    near = dot(onehot(cols_ref[:, 0:1], (tile, own_count), 1), node_ref[...])
    far = dot(onehot(cols_ref[:, 1:2], (tile, slots), 1), rep_ref[...])
    target = cols_ref[:, 2:3].astype(F32)
    product = (near * far).astype(BF)
    near_b = near.astype(BF)
    pre_first = (
        dot(near_b, wf_ref[:width])
        + dot(far.astype(BF), wf_ref[width : 2 * width])
        + dot(product, wf_ref[2 * width :])
    )
    sig = jax.nn.sigmoid(pre_first)
    first = (pre_first * sig).astype(BF)
    slope_first = sig * (1.0 + pre_first * (1.0 - sig))
    first_out[...] = first
    pre_second = dot(first, ws_ref[...])
    sig = jax.nn.sigmoid(pre_second)
    second = (pre_second * sig).astype(BF).astype(F32)
    slope_second = sig * (1.0 + pre_second * (1.0 - sig))
    w_third = wt_ref[...].astype(F32)
    logits = jnp.sum(second * w_third, axis=1, keepdims=True)
    place = step * tile + lax.broadcasted_iota(I32, (tile, 1), 0)
    live = jnp.where(place < live_ref[0], 1.0, 0.0)
    slope = live * (jax.nn.sigmoid(logits) - target)
    softplus = jnp.maximum(logits, 0.0) + jnp.log1p(jnp.exp(-jnp.abs(logits)))
    loss = jnp.sum(live * (softplus - target * logits), axis=0, keepdims=True)
    extra_out[0:1, :hidden2] += scale * jnp.sum(slope * second, axis=0, keepdims=True)
    extra_out[1:2, :hidden2] += jnp.broadcast_to(scale * loss, (1, hidden2))
    back_second = (slope * w_third * slope_second).astype(BF)
    bsecond_out[...] = back_second
    back_first = (dot(back_second, ws_ref[...], 1, 1) * slope_first).astype(BF)
    bfirst_out[...] = back_first
    block_b = dot(back_first, wf_ref[width : 2 * width], 1, 1)
    block_c = dot(back_first, wf_ref[2 * width :], 1, 1)
    high, low = halves(block_b + block_c * near)
    place = onehot(slots_ref[...], (slots, tile), 0)
    acc[...] += dot(place, high) + dot(place, low)

    @pl.when(step == pl.num_programs(0) - 1)
    def _():
        slot_out[...] = acc[...].astype(BF)


def weight_kernel(
    scale, n_edge, edge_ref, lines_ref, node_ref, rep_ref, first_ref, bfirst_ref, bsecond_ref, extra_ref,
    kept_out, sent_out, grads, grads2,
):
    own_count, width = node_ref.shape
    slots = rep_ref.shape[0]
    edges = lines_ref.shape[1]
    chips = n_edge // 2
    rows1 = 3 * width // n_edge
    rows2 = grads2.shape[0] // n_edge
    bfirst = bfirst_ref[...]
    near = dot(node_ref[...], onehot(lines_ref[0:1, :], (own_count, edges), 0), 0, 0)
    grads[:width] = scale * dot(near.astype(BF), bfirst)
    far = dot(rep_ref[...], onehot(lines_ref[1:2, :], (slots, edges), 0), 0, 0)
    grads[width : 2 * width] = scale * dot(far.astype(BF), bfirst)
    grads[2 * width :] = scale * dot((near * far).astype(BF), bfirst)
    grads2[...] = scale * dot(bsecond_ref[...], first_ref[...], 0, 0)
    edge = edge_ref[0]
    chip = edge // 2
    core = edge % 2
    for j in range(chips):
        there = 2 * ((chip + j) % chips)
        for out, owner in ((kept_out, there + core), (sent_out, there + 1 - core)):
            out[j, :rows1] = grads[pl.ds(pl.multiple_of(owner * rows1, 8), rows1), :]
            out[j, rows1 : rows1 + rows2] = grads2[pl.ds(pl.multiple_of(owner * rows2, 8), rows2), :]
            out[j, rows1 + rows2 :] = extra_ref[...]


def near_kernel(lines_ref, cols_ref, rep_ref, bfirst_ref, wf_ref, out_ref):
    edges = lines_ref.shape[1]
    slots, width = rep_ref.shape
    bfirst = bfirst_ref[...]
    far = dot(onehot(cols_ref[:, 1:2], (edges, slots), 1), rep_ref[...])
    block_a = dot(bfirst, wf_ref[:width], 1, 1)
    block_c = dot(bfirst, wf_ref[2 * width :], 1, 1)
    high, low = halves(block_a + block_c * far)
    place = onehot(lines_ref[0:1, :], (out_ref.shape[0], edges), 0)
    out_ref[...] = dot(place, high) + dot(place, low)


def owned_kernel(n_edge, edge_ref, asked_ref, near_ref, back_ref, kept_out, sent_out, total):
    own_count = near_ref.shape[0]
    chips = n_edge // 2
    rows = own_count // n_edge
    place = onehot(asked_ref[...], (own_count, asked_ref.shape[1]), 0)
    total[...] = near_ref[...] + dot(place, back_ref[...])
    edge = edge_ref[0]
    chip = edge // 2
    core = edge % 2
    for j in range(chips):
        there = 2 * ((chip + j) % chips)
        for out, owner in ((kept_out, there + core), (sent_out, there + 1 - core)):
            out[j] = total[pl.ds(pl.multiple_of(owner * rows, 8), rows), :]


def chip_kernel(rows, kept_ref, got_ref, own_out, *packs):
    own_out[...] = kept_ref[0] + got_ref[0]
    for j, out in enumerate(packs):
        high, low = halves(kept_ref[j + 1] + got_ref[j + 1])
        out[: rows + 8] = high
        out[rows + 8 :] = low[rows:]


def total_kernel(parts, n_second, *refs):
    own_ref, gots, out_ref = refs[0], refs[1:-2], refs[-1]
    share = own_ref.shape[1] // parts
    rows = own_ref.shape[0] - 8
    lanes = out_ref.shape[1]
    total = own_ref[...]
    for ref in gots:
        got = ref[...].astype(F32)
        total = total + jnp.concatenate([got[:rows], got[rows : rows + 8] + got[rows + 8 :]], axis=0)
    hidden = total.shape[1]
    turned = jnp.concatenate([total[:rows], jnp.zeros((lanes - rows, hidden), F32)], axis=0).T
    third = total[rows : rows + 1, :n_second]
    loss = total[rows + 1 : rows + 2, :1]
    mine = lax.broadcasted_iota(I32, (hidden, n_second), 0) % share
    mine = mine == lax.broadcasted_iota(I32, (hidden, n_second), 1) % share
    lane = lax.broadcasted_iota(I32, (n_second, lanes), 1) - rows
    group = lax.broadcasted_iota(I32, (n_second, lanes), 0) // share
    groups = n_second // share
    for part, values in enumerate(halves(third)):
        spread = jnp.where(mine, jnp.broadcast_to(values.astype(F32), (hidden, n_second)), 0.0)
        turned = turned + dot(
            spread.astype(BF), jnp.where(lane == group + part * groups, 1.0, 0.0).astype(BF)
        )
    lane = lax.broadcasted_iota(I32, (hidden, lanes), 1) - rows - 2 * groups
    for part, values in enumerate(halves(loss)):
        turned = turned + jnp.where(lane == part, values.astype(F32), 0.0)
    out_ref[...] = turned.astype(BF)


def final_kernel(rows1, rows2, got_ref, first_out, second_out, third_out, loss_out):
    total = jnp.sum(got_ref[...].astype(F32), axis=0)
    share, lanes = total.shape
    rows = rows1 + rows2
    n_second = third_out.shape[1]
    groups = n_second // share
    first_out[...] = total[:, :rows1]
    second_out[...] = total[:, rows1:rows]
    lane = lax.broadcasted_iota(I32, (lanes, n_second), 0) - rows
    group = lax.broadcasted_iota(I32, (lanes, n_second), 1) // share
    take = jnp.where((lane == group) | (lane == group + groups), 1.0, 0.0)
    spread = lax.dot_general(
        total, take, (((1,), (0,)), ((), ())),
        precision=lax.Precision.HIGHEST, preferred_element_type=F32,
    )
    mine = lax.broadcasted_iota(I32, (share, n_second), 0)
    mine = mine == lax.broadcasted_iota(I32, (share, n_second), 1) % share
    third_out[...] = jnp.sum(jnp.where(mine, spread, 0.0), axis=0, keepdims=True)
    place = rows + 2 * groups
    loss_out[...] = total[0:1, place : place + 1] + total[0:1, place + 1 : place + 2]


def body(node_rows, w_first, w_second, w_third, src_row, requests, slot_index, labels, live_count):
    own_count, width = node_rows.shape
    edges = src_row.shape[0]
    parts, cap = requests.shape
    n_edge = lax.axis_size("edge")
    chips = n_edge // 2
    slots = parts * cap
    hidden, hidden2 = w_second.shape
    scale = 1.0 / math.sqrt(edges * parts * n_edge)
    edge = lax.axis_index("edge").astype(I32).reshape(1)
    sibling = [(i, i ^ 1) for i in range(n_edge)]

    def ahead(step):
        return [(i, (i + 2 * step) % n_edge) for i in range(n_edge)]

    steps = (1, chips - 1) + tuple(range(2, chips - 1))
    rows1 = 3 * width // n_edge
    rows2 = hidden2 // n_edge
    rows = rows1 + rows2
    cols = jnp.stack([src_row, slot_index, labels], axis=1)
    lines = jnp.stack([src_row, slot_index], axis=0)

    asked_here = lax.all_to_all(requests, "dom", split_axis=0, concat_axis=0, tiled=True)
    asked_line = asked_here.reshape(1, slots)
    answer = pl.pallas_call(
        answer_kernel,
        out_shape=jax.ShapeDtypeStruct((slots, width), BF),
        in_specs=[WHOLE, WHOLE],
        out_specs=WHOLE,
        compiler_params=params(8),
        name="answer",
    )(asked_line, node_rows)
    replies = lax.all_to_all(
        answer.reshape(parts, cap, width), "dom", split_axis=0, concat_axis=0, tiled=True
    ).reshape(slots, width)

    def fixed(shape):
        return pl.BlockSpec(shape, lambda i: (0,) * len(shape), pipeline_mode=pl.Buffered(1))

    def tiles(count):
        return pl.BlockSpec((TILE, count), lambda i: (i, 0))

    slot_grad, first, back_first, back_second, extra = pl.pallas_call(
        functools.partial(pair_kernel, scale),
        grid=(edges // TILE,),
        out_shape=(
            jax.ShapeDtypeStruct((slots, width), BF),
            jax.ShapeDtypeStruct((edges, hidden), BF),
            jax.ShapeDtypeStruct((edges, hidden), BF),
            jax.ShapeDtypeStruct((edges, hidden2), BF),
            jax.ShapeDtypeStruct((8, hidden), F32),
        ),
        in_specs=[
            SCALARS,
            tiles(3),
            pl.BlockSpec((1, TILE), lambda i: (0, i)),
            fixed((own_count, width)),
            fixed((slots, width)),
            fixed((3 * width, hidden)),
            fixed((hidden, hidden2)),
            fixed((1, hidden2)),
        ],
        out_specs=(
            pl.BlockSpec((slots, width), lambda i: (0, 0)),
            tiles(hidden),
            tiles(hidden),
            tiles(hidden2),
            pl.BlockSpec((8, hidden), lambda i: (0, 0)),
        ),
        scratch_shapes=[pltpu.VMEM((slots, width), F32)],
        compiler_params=params(32),
        cost_estimate=cost(6 * 10**9, 8 * MIB),
        name="pair",
    )(
        live_count, cols, slot_index.reshape(1, edges), node_rows, replies, w_first, w_second,
        w_third.reshape(1, hidden2),
    )

    returned = lax.all_to_all(
        slot_grad.reshape(parts, cap, width), "dom", split_axis=0, concat_axis=0, tiled=True
    ).reshape(slots, width)

    block = jax.ShapeDtypeStruct((chips, rows + 8, hidden), F32)
    kept, sent = pl.pallas_call(
        functools.partial(weight_kernel, scale, n_edge),
        out_shape=(block, block),
        in_specs=[SCALARS] + [WHOLE] * 7,
        out_specs=(WHOLE, WHOLE),
        scratch_shapes=[pltpu.VMEM((3 * width, hidden), F32), pltpu.VMEM((hidden2, hidden), F32)],
        compiler_params=params(32),
        cost_estimate=FREE,
        name="weights",
    )(edge, lines, node_rows, replies, first, back_first, back_second, extra)
    pack = jax.ShapeDtypeStruct((rows + 16, hidden), BF)
    own, *packs = pl.pallas_call(
        functools.partial(chip_kernel, rows),
        out_shape=(jax.ShapeDtypeStruct((rows + 8, hidden), F32),) + (pack,) * (chips - 1),
        in_specs=[WHOLE] * 2,
        out_specs=(WHOLE,) * chips,
        compiler_params=params(16),
        cost_estimate=FREE,
        name="chip",
    )(kept, lax.ppermute(sent, "edge", sibling))
    gots = [lax.ppermute(packs[step - 1], "edge", ahead(step)) for step in steps]

    near_part = pl.pallas_call(
        near_kernel,
        out_shape=jax.ShapeDtypeStruct((own_count, width), F32),
        in_specs=[WHOLE] * 5,
        out_specs=WHOLE,
        compiler_params=params(32),
        cost_estimate=FREE,
        name="near",
    )(lines, cols, replies, back_first, w_first)

    share = hidden // parts
    lanes = -(-(rows + 2 * (hidden2 // share) + 2) // 128) * 128
    packed = pl.pallas_call(
        functools.partial(total_kernel, parts, hidden2),
        out_shape=jax.ShapeDtypeStruct((hidden, lanes), BF),
        in_specs=[WHOLE] * chips + [pl.BlockSpec(memory_space=pl.ANY)],
        out_specs=WHOLE,
        compiler_params=params(16),
        cost_estimate=FREE,
        name="total",
    )(own, *gots, near_part)
    got = lax.all_to_all(
        packed.reshape(parts, share, lanes), "dom", split_axis=0, concat_axis=0, tiled=True
    )
    first_t, second_share, third_total, loss_total = pl.pallas_call(
        functools.partial(final_kernel, rows1, rows2),
        out_shape=(
            jax.ShapeDtypeStruct((share, rows1), F32),
            jax.ShapeDtypeStruct((share, rows2), F32),
            jax.ShapeDtypeStruct((1, hidden2), F32),
            jax.ShapeDtypeStruct((1, 1), F32),
        ),
        in_specs=[WHOLE],
        out_specs=(WHOLE,) * 4,
        compiler_params=params(8),
        cost_estimate=FREE,
        name="final",
    )(got)

    block = jax.ShapeDtypeStruct((chips, own_count // n_edge, width), F32)
    kept, sent = pl.pallas_call(
        functools.partial(owned_kernel, n_edge),
        out_shape=(block, block),
        in_specs=[SCALARS] + [WHOLE] * 3,
        out_specs=(WHOLE, WHOLE),
        scratch_shapes=[pltpu.VMEM((own_count, width), F32)],
        compiler_params=params(8),
        cost_estimate=FREE,
        name="owned",
    )(edge, asked_line, near_part, returned)
    node_chip = kept + lax.ppermute(sent, "edge", sibling)
    node_share = node_chip[0]
    for step in steps:
        node_share = node_share + lax.ppermute(node_chip[step], "edge", ahead(step))
    return (
        first_t.T, second_share, third_total.reshape(hidden2), loss_total.reshape(()), node_share
    )


def solution(mesh):
    in_specs = (
        P("dom", None),
        P(),
        P(),
        P(),
        P(("dom", "edge")),
        P(("dom", "edge"), None),
        P(("dom", "edge")),
        P(("dom", "edge")),
        P(("dom", "edge")),
    )
    out_specs = (P("edge", "dom"), P("dom", "edge"), P(), P(), P(("dom", "edge"), None))
    return jax.shard_map(body, mesh=mesh, in_specs=in_specs, out_specs=out_specs, check_vma=False)
```

```python
import functools
import math

import jax
import jax.numpy as jnp
from jax import lax
from jax.experimental import pallas as pl
from jax.experimental.pallas import tpu as pltpu
from jax.sharding import PartitionSpec as P

BF = jnp.bfloat16
F32 = jnp.float32
I32 = jnp.int32
MIB = 1 << 20
TILE = 512
LAST = 0
WHOLE = pl.BlockSpec(memory_space=pltpu.VMEM)
FREE = pl.CostEstimate(flops=0, bytes_accessed=0, transcendentals=0)
ANYWHERE = pl.BlockSpec(memory_space=pl.ANY)
FAR = pl.BlockSpec(memory_space=pltpu.HBM)
SCALARS = pl.BlockSpec(memory_space=pltpu.SMEM)


def dot(left, right, left_dim=1, right_dim=0):
    return lax.dot_general(
        left, right, (((left_dim,), (right_dim,)), ((), ())), preferred_element_type=F32
    )


def halves(values):
    high = values.astype(BF)
    return high, (values - high.astype(F32)).astype(BF)


def ring_mask(j):
    return (0, 3, 1, 2)[j]


def onehot(index, shape, axis):
    return jnp.where(index == lax.broadcasted_iota(I32, shape, axis), 1.0, 0.0).astype(BF)


def params(mib):
    return pltpu.CompilerParams(vmem_limit_bytes=mib * MIB)


def cost(flops, nbytes):
    return pl.CostEstimate(flops=flops, bytes_accessed=nbytes, transcendentals=0)


def answer_kernel(asked_ref, node_any, out_ref, line_out, node_ref, sem):
    fetch = pltpu.make_async_copy(node_any, node_ref, sem)
    fetch.start()
    parts, cap = asked_ref.shape
    own_count, slots = node_ref.shape[0], line_out.shape[1]
    spread = lax.broadcasted_iota(I32, (parts, slots), 0)
    spread = spread == lax.broadcasted_iota(I32, (parts, slots), 1) // cap
    lines = dot(asked_ref[...].astype(F32).astype(BF), jnp.where(spread, 1.0, 0.0).astype(BF), 0, 0)
    mine = lax.broadcasted_iota(I32, (cap, slots), 0)
    mine = mine == lax.broadcasted_iota(I32, (cap, slots), 1) % cap
    line = jnp.sum(jnp.where(mine, lines, 0.0), axis=0, keepdims=True).astype(I32)
    line_out[...] = line
    pick = onehot(line, (own_count, slots), 0)
    fetch.wait()
    out_ref[...] = dot(pick, node_ref[...], 0, 0).astype(BF)


def pair_kernel(
    scale, live_ref, cols_ref, slots_ref, node_ref, rep_ref, wf_any, ws_ref, wt_ref,
    slot_out, first_out, bfirst_out, bsecond_out, extra_out, acc, wf_ref, sem,
):
    step = pl.program_id(0)
    tile = cols_ref.shape[0]
    own_count, width = node_ref.shape
    slots = rep_ref.shape[0]
    hidden2 = ws_ref.shape[1]

    fetch = [
        pltpu.make_async_copy(wf_any.at[pl.ds(i * width, width)], wf_ref.at[pl.ds(i * width, width)], sem.at[i])
        for i in range(3)
    ]

    def arrive(i):
        @pl.when(step == 0)
        def _():
            fetch[i].wait()

    @pl.when(step == 0)
    def _():
        for copy in fetch:
            copy.start()
        acc[...] = jnp.zeros_like(acc)
        extra_out[...] = jnp.zeros_like(extra_out)

    near = dot(onehot(cols_ref[:, 0:1], (tile, own_count), 1), node_ref[...])
    far = dot(onehot(cols_ref[:, 1:2], (tile, slots), 1), rep_ref[...])
    target = cols_ref[:, 2:3].astype(F32)
    product = (near * far).astype(BF)
    near_b = near.astype(BF)
    arrive(0)
    pre_first = dot(near_b, wf_ref[:width])
    arrive(1)
    pre_first = pre_first + dot(far.astype(BF), wf_ref[width : 2 * width])
    arrive(2)
    pre_first = pre_first + dot(product, wf_ref[2 * width :])
    sig = jax.nn.sigmoid(pre_first)
    first = (pre_first * sig).astype(BF)
    slope_first = sig * (1.0 + pre_first * (1.0 - sig))
    first_out[...] = first
    pre_second = dot(first, ws_ref[...])
    sig = jax.nn.sigmoid(pre_second)
    second = (pre_second * sig).astype(BF).astype(F32)
    slope_second = sig * (1.0 + pre_second * (1.0 - sig))
    w_third = wt_ref[...].astype(F32)
    logits = jnp.sum(second * w_third, axis=1, keepdims=True)
    place = step * tile + lax.broadcasted_iota(I32, (tile, 1), 0)
    live = jnp.where(place < live_ref[0], 1.0, 0.0)
    slope = live * (jax.nn.sigmoid(logits) - target)
    softplus = jnp.maximum(logits, 0.0) + jnp.log1p(jnp.exp(-jnp.abs(logits)))
    loss = jnp.sum(live * (softplus - target * logits), axis=0, keepdims=True)
    extra_out[0:1, :hidden2] += scale * jnp.sum(slope * second, axis=0, keepdims=True)
    extra_out[1:2, :hidden2] += jnp.broadcast_to(scale * loss, (1, hidden2))
    back_second = (slope * w_third * slope_second).astype(BF)
    bsecond_out[...] = back_second
    back_first = (dot(back_second, ws_ref[...], 1, 1) * slope_first).astype(BF)
    bfirst_out[...] = back_first
    block_b = dot(back_first, wf_ref[width : 2 * width], 1, 1)
    block_c = dot(back_first, wf_ref[2 * width :], 1, 1)
    high, low = halves(block_b + block_c * near)
    place = onehot(slots_ref[...], (slots, tile), 0)
    acc[...] += dot(place, high) + dot(place, low)

    @pl.when(step == pl.num_programs(0) - 1)
    def _():
        slot_out[...] = acc[...].astype(BF)


def weight_kernel(
    scale, n_edge, edge_ref, lines_ref, node_any, rep_any, first_any, bfirst_any, bsecond_any, extra_ref,
    kept_out, sent_out, grads, grads2, node_ref, rep_ref, first_ref, bfirst_ref, bsecond_ref, sems,
):
    pairs = (
        (node_any, node_ref), (rep_any, rep_ref), (bfirst_any, bfirst_ref), (bsecond_any, bsecond_ref),
        (first_any, first_ref),
    )
    fetch = [pltpu.make_async_copy(src, dst, sems.at[i]) for i, (src, dst) in enumerate(pairs)]
    for copy in fetch:
        copy.start()
    own_count, width = node_ref.shape
    slots = rep_ref.shape[0]
    edges = lines_ref.shape[1]
    rows1 = 3 * width // n_edge
    rows2 = grads2.shape[0] // n_edge
    rows = rows1 + rows2
    fetch[0].wait()
    near = dot(node_ref[...], onehot(lines_ref[0:1, :], (own_count, edges), 0), 0, 0)
    fetch[1].wait()
    far = dot(rep_ref[...], onehot(lines_ref[1:2, :], (slots, edges), 0), 0, 0)
    fetch[2].wait()
    bfirst = bfirst_ref[...]
    grads[:width] = scale * dot(near.astype(BF), bfirst)
    grads[width : 2 * width] = scale * dot(far.astype(BF), bfirst)
    grads[2 * width :] = scale * dot((near * far).astype(BF), bfirst)
    fetch[3].wait()
    fetch[4].wait()
    grads2[...] = scale * dot(bsecond_ref[...], first_ref[...], 0, 0)
    edge = edge_ref[0]
    chip = edge // 2
    core = edge % 2
    chips = n_edge // 2
    extra = extra_ref[...]
    extra_high, extra_low = halves(extra)
    for j in range(chips):
        owner = 2 * ((chip + j) % chips) + core
        kept_out[j, :rows1] = grads[pl.ds(pl.multiple_of(owner * rows1, 8), rows1), :]
        kept_out[j, rows1:rows] = grads2[pl.ds(pl.multiple_of(owner * rows2, 8), rows2), :]
        kept_out[j, rows:] = extra
        owner = 2 * ((chip + j) % chips) + 1 - core
        sent_out[j, :rows1] = grads[pl.ds(pl.multiple_of(owner * rows1, 8), rows1), :].astype(BF)
        sent_out[j, rows1:rows] = grads2[pl.ds(pl.multiple_of(owner * rows2, 8), rows2), :].astype(BF)
        sent_out[j, rows:] = jnp.concatenate([extra_high, extra_low], axis=0)


def near_kernel(lines_ref, cols_ref, rep_ref, bfirst_ref, wf_ref, out_ref):
    edges = lines_ref.shape[1]
    slots, width = rep_ref.shape
    bfirst = bfirst_ref[...]
    far = dot(onehot(cols_ref[:, 1:2], (edges, slots), 1), rep_ref[...])
    block_a = dot(bfirst, wf_ref[:width], 1, 1)
    block_c = dot(bfirst, wf_ref[2 * width :], 1, 1)
    high, low = halves(block_a + block_c * far)
    place = onehot(lines_ref[0:1, :], (out_ref.shape[0], edges), 0)
    out_ref[...] = dot(place, high) + dot(place, low)


def owned_kernel(n_edge, edge_ref, asked_ref, near_ref, back_ref, packed_ref, kept_out, sent_out, packed_out, total):
    own_count = near_ref.shape[0]
    rows = own_count // n_edge
    place = onehot(asked_ref[...], (own_count, asked_ref.shape[1]), 0)
    total[...] = near_ref[...] + dot(place, back_ref[...])
    edge = edge_ref[0]
    for j in range(n_edge // 2):
        mask = ring_mask(j)
        owner = edge ^ (2 * mask)
        for out, who in ((kept_out, owner), (sent_out, owner ^ 1)):
            out[j] = total[pl.ds(pl.multiple_of(who * rows, 8), rows), :]


def add_kernel(kept_ref, got_ref, kept_out, sent_out):
    half = kept_out.shape[0]
    kept_out[...] = kept_ref[:half] + got_ref[:half].astype(F32)
    sent_out[...] = (kept_ref[half:] + got_ref[half:].astype(F32)).astype(BF)


def last_kernel(kept_ref, got_ref, out_ref):
    out_ref[...] = kept_ref[0] + got_ref[0].astype(F32)


def widen(packed, rows):
    values = packed.astype(F32)
    return jnp.concatenate([values[:rows], values[rows : rows + 8] + values[rows + 8 :]], axis=0)


def chip_kernel(rows, kept_ref, got_ref, own_out, *packs):
    own_out[...] = kept_ref[0] + widen(got_ref[0], rows)
    for j, out in enumerate(packs):
        high, low = halves(kept_ref[j + 1] + widen(got_ref[j + 1], rows))
        out[: rows + 8] = high
        out[rows + 8 :] = low[rows:]


def total_kernel(parts, n_second, *refs):
    own_ref, gots, out_ref = refs[0], refs[1:-2], refs[-1]
    share = own_ref.shape[1] // parts
    rows = own_ref.shape[0] - 8
    lanes = out_ref.shape[1]
    total = own_ref[...]
    for ref in gots:
        total = total + widen(ref[...], rows)
    hidden = total.shape[1]
    turned = jnp.concatenate([total[:rows], jnp.zeros((lanes - rows, hidden), F32)], axis=0).T
    third = total[rows : rows + 1, :n_second]
    loss = total[rows + 1 : rows + 2, :1]
    mine = lax.broadcasted_iota(I32, (hidden, n_second), 0) % share
    mine = mine == lax.broadcasted_iota(I32, (hidden, n_second), 1) % share
    lane = lax.broadcasted_iota(I32, (n_second, lanes), 1) - rows
    group = lax.broadcasted_iota(I32, (n_second, lanes), 0) // share
    groups = n_second // share
    for part, values in enumerate(halves(third)):
        spread = jnp.where(mine, jnp.broadcast_to(values.astype(F32), (hidden, n_second)), 0.0)
        turned = turned + dot(
            spread.astype(BF), jnp.where(lane == group + part * groups, 1.0, 0.0).astype(BF)
        )
    lane = lax.broadcasted_iota(I32, (hidden, lanes), 1) - rows - 2 * groups
    for part, values in enumerate(halves(loss)):
        turned = turned + jnp.where(lane == part, values.astype(F32), 0.0)
    out_ref[...] = turned.astype(BF)


def final_kernel(rows1, rows2, got_ref, first_out, second_out, third_out, loss_out):
    total = jnp.sum(got_ref[...].astype(F32), axis=0)
    share, lanes = total.shape
    rows = rows1 + rows2
    n_second = third_out.shape[1]
    groups = n_second // share
    first_out[...] = total[:, :rows1]
    second_out[...] = total[:, rows1:rows]
    lane = lax.broadcasted_iota(I32, (lanes, n_second), 0) - rows
    group = lax.broadcasted_iota(I32, (lanes, n_second), 1) // share
    take = jnp.where((lane == group) | (lane == group + groups), 1.0, 0.0)
    spread = lax.dot_general(
        total, take, (((1,), (0,)), ((), ())),
        precision=lax.Precision.HIGHEST, preferred_element_type=F32,
    )
    mine = lax.broadcasted_iota(I32, (share, n_second), 0)
    mine = mine == lax.broadcasted_iota(I32, (share, n_second), 1) % share
    third_out[...] = jnp.sum(jnp.where(mine, spread, 0.0), axis=0, keepdims=True)
    place = rows + 2 * groups
    loss_out[...] = total[0:1, place : place + 1] + total[0:1, place + 1 : place + 2]


def body(node_rows, w_first, w_second, w_third, src_row, requests, slot_index, labels, live_count):
    own_count, width = node_rows.shape
    edges = src_row.shape[0]
    parts, cap = requests.shape
    n_edge = lax.axis_size("edge")
    chips = n_edge // 2
    slots = parts * cap
    hidden, hidden2 = w_second.shape
    scale = 1.0 / math.sqrt(edges * parts * n_edge)
    edge = lax.axis_index("edge").astype(I32).reshape(1)
    sibling = [(i, i ^ 1) for i in range(n_edge)]

    def ahead(step):
        return [(i, (i + 2 * step) % n_edge) for i in range(n_edge)]

    steps = tuple(range(2, chips - 1)) + (1, chips - 1)
    rows1 = 3 * width // n_edge
    rows2 = hidden2 // n_edge
    rows = rows1 + rows2
    cols = jnp.stack([src_row, slot_index, labels], axis=1)
    lines = jnp.stack([src_row, slot_index], axis=0)

    asked_here = lax.all_to_all(requests, "dom", split_axis=0, concat_axis=0, tiled=True)
    answer, asked_line = pl.pallas_call(
        answer_kernel,
        out_shape=(
            jax.ShapeDtypeStruct((slots, width), BF),
            jax.ShapeDtypeStruct((1, slots), I32),
        ),
        in_specs=[WHOLE, FAR],
        out_specs=(WHOLE, WHOLE),
        scratch_shapes=[pltpu.VMEM((own_count, width), BF), pltpu.SemaphoreType.DMA],
        compiler_params=params(8),
        name="answer",
    )(asked_here, node_rows)
    replies = lax.all_to_all(
        answer.reshape(parts, cap, width), "dom", split_axis=0, concat_axis=0, tiled=True
    ).reshape(slots, width)

    def fixed(shape):
        return pl.BlockSpec(shape, lambda i: (0,) * len(shape), pipeline_mode=pl.Buffered(1))

    def tiles(count):
        return pl.BlockSpec((TILE, count), lambda i: (i, 0))

    slot_grad, first, back_first, back_second, extra = pl.pallas_call(
        functools.partial(pair_kernel, scale),
        grid=(edges // TILE,),
        out_shape=(
            pltpu.HBM((slots, width), BF),
            pltpu.HBM((edges, hidden), BF),
            pltpu.HBM((edges, hidden), BF),
            pltpu.HBM((edges, hidden2), BF),
            jax.ShapeDtypeStruct((8, hidden), F32),
        ),
        in_specs=[
            SCALARS,
            tiles(3),
            pl.BlockSpec((1, TILE), lambda i: (0, i)),
            fixed((own_count, width)),
            fixed((slots, width)),
            FAR,
            fixed((hidden, hidden2)),
            fixed((1, hidden2)),
        ],
        out_specs=(
            pl.BlockSpec((slots, width), lambda i: (0, 0)),
            tiles(hidden),
            tiles(hidden),
            tiles(hidden2),
            pl.BlockSpec((8, hidden), lambda i: (0, 0)),
        ),
        scratch_shapes=[
            pltpu.VMEM((slots, width), F32),
            pltpu.VMEM((3 * width, hidden), BF),
            pltpu.SemaphoreType.DMA((3,)),
        ],
        compiler_params=params(32),
        cost_estimate=cost(6 * 10**9, 8 * MIB),
        name="pair",
    )(
        live_count, cols, slot_index.reshape(1, edges), node_rows, replies, w_first, w_second,
        w_third.reshape(1, hidden2),
    )

    returned = lax.all_to_all(
        slot_grad.reshape(parts, cap, width), "dom", split_axis=0, concat_axis=0, tiled=True
    ).reshape(slots, width)

    kept, sent = pl.pallas_call(
        functools.partial(weight_kernel, scale, n_edge),
        out_shape=(
            jax.ShapeDtypeStruct((chips, rows + 8, hidden), F32),
            jax.ShapeDtypeStruct((chips, rows + 16, hidden), BF),
        ),
        in_specs=[SCALARS, WHOLE] + [FAR] * 5 + [WHOLE],
        out_specs=(WHOLE, WHOLE),
        scratch_shapes=[
            pltpu.VMEM((3 * width, hidden), F32),
            pltpu.VMEM((hidden2, hidden), F32),
            pltpu.VMEM((own_count, width), BF),
            pltpu.VMEM((slots, width), BF),
            pltpu.VMEM((edges, hidden), BF),
            pltpu.VMEM((edges, hidden), BF),
            pltpu.VMEM((edges, hidden2), BF),
            pltpu.SemaphoreType.DMA((5,)),
        ],
        compiler_params=params(32),
        cost_estimate=FREE,
        name="weights",
    )(edge, lines, node_rows, replies, first, back_first, back_second, extra)
    near_part = pl.pallas_call(
        near_kernel,
        out_shape=jax.ShapeDtypeStruct((own_count, width), F32),
        in_specs=[WHOLE] * 5,
        out_specs=WHOLE,
        compiler_params=params(32),
        cost_estimate=FREE,
        name="near",
    )(lines, cols, replies, back_first, w_first)

    pack = jax.ShapeDtypeStruct((rows + 16, hidden), BF)
    own, *packs = pl.pallas_call(
        functools.partial(chip_kernel, rows),
        out_shape=(jax.ShapeDtypeStruct((rows + 8, hidden), F32),) + (pack,) * (chips - 1),
        in_specs=[WHOLE] * 2,
        out_specs=(WHOLE,) * chips,
        compiler_params=params(16),
        cost_estimate=FREE,
        name="chip",
    )(kept, lax.ppermute(sent, "edge", sibling))
    gots = [lax.ppermute(packs[step - 1], "edge", ahead(step)) for step in steps]

    share = hidden // parts
    lanes = -(-(rows + 2 * (hidden2 // share) + 2) // 128) * 128
    packed = pl.pallas_call(
        functools.partial(total_kernel, parts, hidden2),
        out_shape=jax.ShapeDtypeStruct((hidden, lanes), BF),
        in_specs=[WHOLE] * chips + [ANYWHERE],
        out_specs=WHOLE,
        compiler_params=params(16),
        cost_estimate=FREE,
        name="total",
    )(own, *gots, near_part)
    block = jax.ShapeDtypeStruct((chips, own_count // n_edge, width), F32)
    kept, sent, packed = pl.pallas_call(
        functools.partial(owned_kernel, n_edge),
        out_shape=(block, block, jax.ShapeDtypeStruct(packed.shape, BF)),
        in_specs=[SCALARS] + [WHOLE] * 3 + [ANYWHERE],
        out_specs=(WHOLE, WHOLE, ANYWHERE),
        input_output_aliases={4: 2},
        scratch_shapes=[pltpu.VMEM((own_count, width), F32)],
        compiler_params=params(8),
        cost_estimate=FREE,
        name="owned",
    )(edge, asked_line, near_part, returned, packed)
    got = lax.all_to_all(
        packed.reshape(parts, share, lanes), "dom", split_axis=0, concat_axis=0, tiled=True
    )
    first_t, second_share, third_total, loss_total = pl.pallas_call(
        functools.partial(final_kernel, rows1, rows2),
        out_shape=(
            jax.ShapeDtypeStruct((share, rows1), F32),
            jax.ShapeDtypeStruct((share, rows2), F32),
            jax.ShapeDtypeStruct((1, hidden2), F32),
            jax.ShapeDtypeStruct((1, 1), F32),
        ),
        in_specs=[WHOLE],
        out_specs=(WHOLE,) * 4,
        compiler_params=params(8),
        cost_estimate=FREE,
        name="final",
    )(got)

    for mask in (0, 1, 3):
        partner = sibling if mask == 0 else [(i, i ^ (2 * mask)) for i in range(n_edge)]
        got = lax.ppermute(sent, "edge", partner)
        if mask == 3:
            break
        half = (kept.shape[0] // 2,) + kept.shape[1:]
        kept, sent = pl.pallas_call(
            add_kernel,
            out_shape=(jax.ShapeDtypeStruct(half, F32), jax.ShapeDtypeStruct(half, BF)),
            in_specs=[WHOLE] * 2,
            out_specs=(WHOLE,) * 2,
            compiler_params=params(8),
            cost_estimate=FREE,
            name="add",
        )(kept, got)
    node_share = pl.pallas_call(
        last_kernel,
        out_shape=jax.ShapeDtypeStruct(kept.shape[1:], F32),
        in_specs=[WHOLE] * 2,
        out_specs=WHOLE,
        compiler_params=params(8),
        cost_estimate=cost(LAST, 0),
        name="last",
    )(kept, got)
    return (
        first_t.T, second_share, third_total.reshape(hidden2), loss_total.reshape(()), node_share
    )


def solution(mesh):
    in_specs = (
        P("dom", None),
        P(),
        P(),
        P(),
        P(("dom", "edge")),
        P(("dom", "edge"), None),
        P(("dom", "edge")),
        P(("dom", "edge")),
        P(("dom", "edge")),
    )
    out_specs = (P("edge", "dom"), P("dom", "edge"), P(), P(), P(("dom", "edge"), None))
    return jax.shard_map(body, mesh=mesh, in_specs=in_specs, out_specs=out_specs, check_vma=False)
```

```python
import functools
import math

import jax
import jax.numpy as jnp
from jax import lax
from jax.experimental import pallas as pl
from jax.experimental.pallas import tpu as pltpu
from jax.sharding import PartitionSpec as P

BF = jnp.bfloat16
F32 = jnp.float32
I32 = jnp.int32
MIB = 1 << 20
TILE = 512
LAST = 0
WHOLE = pl.BlockSpec(memory_space=pltpu.VMEM)
FREE = pl.CostEstimate(flops=0, bytes_accessed=0, transcendentals=0)
ANYWHERE = pl.BlockSpec(memory_space=pl.ANY)
FAR = pl.BlockSpec(memory_space=pltpu.HBM)
SCALARS = pl.BlockSpec(memory_space=pltpu.SMEM)


def dot(left, right, left_dim=1, right_dim=0):
    return lax.dot_general(
        left, right, (((left_dim,), (right_dim,)), ((), ())), preferred_element_type=F32
    )


def halves(values):
    high = values.astype(BF)
    return high, (values - high.astype(F32)).astype(BF)


def ring_mask(j):
    return (0, 3, 1, 2)[j]


def onehot(index, shape, axis):
    return jnp.where(index == lax.broadcasted_iota(I32, shape, axis), 1.0, 0.0).astype(BF)


def params(mib):
    return pltpu.CompilerParams(vmem_limit_bytes=mib * MIB)


def in_hbm(array):
    return pltpu.with_memory_space_constraint(array, pltpu.HBM)


def cost(flops, nbytes):
    return pl.CostEstimate(flops=flops, bytes_accessed=nbytes, transcendentals=0)


def answer_kernel(asked_ref, node_any, out_ref, line_out, node_ref, sem):
    fetch = pltpu.make_async_copy(node_any, node_ref, sem)
    fetch.start()
    parts, cap = asked_ref.shape
    own_count, slots = node_ref.shape[0], line_out.shape[1]
    spread = lax.broadcasted_iota(I32, (parts, slots), 0)
    spread = spread == lax.broadcasted_iota(I32, (parts, slots), 1) // cap
    lines = dot(asked_ref[...].astype(F32).astype(BF), jnp.where(spread, 1.0, 0.0).astype(BF), 0, 0)
    mine = lax.broadcasted_iota(I32, (cap, slots), 0)
    mine = mine == lax.broadcasted_iota(I32, (cap, slots), 1) % cap
    line = jnp.sum(jnp.where(mine, lines, 0.0), axis=0, keepdims=True).astype(I32)
    line_out[...] = line
    pick = onehot(line, (own_count, slots), 0)
    fetch.wait()
    out_ref[...] = dot(pick, node_ref[...], 0, 0).astype(BF)


def pair_kernel(
    scale, live_ref, cols_ref, slots_ref, node_ref, rep_ref, wf_any, ws_ref, wt_ref,
    slot_out, first_out, bfirst_out, bsecond_out, extra_out,
    wf_ref, slot_ref, first_ref, bfirst_ref, bsecond_ref, fetch_sems, store_sems,
):
    edges = cols_ref.shape[0]
    own_count, width = node_ref.shape
    slots = rep_ref.shape[0]
    hidden2 = ws_ref.shape[1]
    fetch = []
    for i in range(3):
        part = pl.ds(i * width, width)
        fetch.append(pltpu.make_async_copy(wf_any.at[part], wf_ref.at[part], fetch_sems.at[i]))
        fetch[-1].start()
    stores = []

    def store(src, dst):
        copy = pltpu.make_async_copy(src, dst, store_sems.at[len(stores)])
        copy.start()
        stores.append(copy)

    w_third = wt_ref[...].astype(F32)
    total = None
    third = None
    loss = None
    for tile in range(edges // TILE):
        part = pl.ds(tile * TILE, TILE)
        near = dot(onehot(cols_ref[part, 0:1], (TILE, own_count), 1), node_ref[...])
        far = dot(onehot(cols_ref[part, 1:2], (TILE, slots), 1), rep_ref[...])
        target = cols_ref[part, 2:3].astype(F32)
        blocks = (near.astype(BF), far.astype(BF), (near * far).astype(BF))
        pre_first = None
        for i, block in enumerate(blocks):
            if tile == 0:
                fetch[i].wait()
            term = dot(block, wf_ref[i * width : (i + 1) * width])
            pre_first = term if pre_first is None else pre_first + term
        sig = jax.nn.sigmoid(pre_first)
        first = (pre_first * sig).astype(BF)
        slope_first = sig * (1.0 + pre_first * (1.0 - sig))
        first_ref[part] = first
        store(first_ref.at[part], first_out.at[part])
        pre_second = dot(first, ws_ref[...])
        sig = jax.nn.sigmoid(pre_second)
        second = (pre_second * sig).astype(BF).astype(F32)
        slope_second = sig * (1.0 + pre_second * (1.0 - sig))
        logits = jnp.sum(second * w_third, axis=1, keepdims=True)
        place = tile * TILE + lax.broadcasted_iota(I32, (TILE, 1), 0)
        live = jnp.where(place < live_ref[0], 1.0, 0.0)
        slope = live * (jax.nn.sigmoid(logits) - target)
        back_second = (slope * w_third * slope_second).astype(BF)
        bsecond_ref[part] = back_second
        store(bsecond_ref.at[part], bsecond_out.at[part])
        back_first = (dot(back_second, ws_ref[...], 1, 1) * slope_first).astype(BF)
        bfirst_ref[part] = back_first
        store(bfirst_ref.at[part], bfirst_out.at[part])
        block_b = dot(back_first, wf_ref[width : 2 * width], 1, 1)
        block_c = dot(back_first, wf_ref[2 * width :], 1, 1)
        high, low = halves(block_b + block_c * near)
        place = onehot(slots_ref[:, part], (slots, TILE), 0)
        term = dot(place, high) + dot(place, low)
        total = term if total is None else total + term
        softplus = jnp.maximum(logits, 0.0) + jnp.log1p(jnp.exp(-jnp.abs(logits)))
        term = jnp.sum(live * (softplus - target * logits), axis=0, keepdims=True)
        loss = term if loss is None else loss + term
        term = jnp.sum(slope * second, axis=0, keepdims=True)
        third = term if third is None else third + term
    slot_ref[...] = total.astype(BF)
    store(slot_ref, slot_out)
    extra_out[...] = jnp.zeros_like(extra_out)
    extra_out[0:1, :hidden2] = scale * third
    extra_out[1:2, :hidden2] = jnp.broadcast_to(scale * loss, (1, hidden2))
    for copy in stores:
        copy.wait()


def weight_kernel(
    scale, n_edge, edge_ref, lines_ref, node_any, rep_any, first_any, bfirst_any, bsecond_any, extra_ref,
    kept_out, sent_out, grads, grads2, node_ref, rep_ref, first_ref, bfirst_ref, bsecond_ref, sems,
):
    pairs = (
        (node_any, node_ref), (rep_any, rep_ref), (bfirst_any, bfirst_ref), (bsecond_any, bsecond_ref),
        (first_any, first_ref),
    )
    fetch = [pltpu.make_async_copy(src, dst, sems.at[i]) for i, (src, dst) in enumerate(pairs)]
    for copy in fetch:
        copy.start()
    own_count, width = node_ref.shape
    slots = rep_ref.shape[0]
    edges = lines_ref.shape[1]
    rows1 = 3 * width // n_edge
    rows2 = grads2.shape[0] // n_edge
    rows = rows1 + rows2
    near_pick = onehot(lines_ref[0:1, :], (own_count, edges), 0)
    far_pick = onehot(lines_ref[1:2, :], (slots, edges), 0)
    fetch[0].wait()
    near = dot(node_ref[...], near_pick, 0, 0)
    fetch[1].wait()
    far = dot(rep_ref[...], far_pick, 0, 0)
    fetch[2].wait()
    bfirst = bfirst_ref[...]
    grads[:width] = scale * dot(near.astype(BF), bfirst)
    grads[width : 2 * width] = scale * dot(far.astype(BF), bfirst)
    grads[2 * width :] = scale * dot((near * far).astype(BF), bfirst)
    fetch[3].wait()
    fetch[4].wait()
    grads2[...] = scale * dot(bsecond_ref[...], first_ref[...], 0, 0)
    edge = edge_ref[0]
    chip = edge // 2
    core = edge % 2
    chips = n_edge // 2
    extra = extra_ref[...]
    extra_high, extra_low = halves(extra)
    for j in range(chips):
        owner = 2 * ((chip + j) % chips) + core
        kept_out[j, :rows1] = grads[pl.ds(pl.multiple_of(owner * rows1, 8), rows1), :]
        kept_out[j, rows1:rows] = grads2[pl.ds(pl.multiple_of(owner * rows2, 8), rows2), :]
        kept_out[j, rows:] = extra
        owner = 2 * ((chip + j) % chips) + 1 - core
        sent_out[j, :rows1] = grads[pl.ds(pl.multiple_of(owner * rows1, 8), rows1), :].astype(BF)
        sent_out[j, rows1:rows] = grads2[pl.ds(pl.multiple_of(owner * rows2, 8), rows2), :].astype(BF)
        sent_out[j, rows:] = jnp.concatenate([extra_high, extra_low], axis=0)


def near_kernel(lines_ref, cols_ref, rep_ref, bfirst_ref, wf_ref, out_ref):
    edges = lines_ref.shape[1]
    slots, width = rep_ref.shape
    bfirst = bfirst_ref[...]
    far = dot(onehot(cols_ref[:, 1:2], (edges, slots), 1), rep_ref[...])
    block_a = dot(bfirst, wf_ref[:width], 1, 1)
    block_c = dot(bfirst, wf_ref[2 * width :], 1, 1)
    high, low = halves(block_a + block_c * far)
    place = onehot(lines_ref[0:1, :], (out_ref.shape[0], edges), 0)
    out_ref[...] = dot(place, high) + dot(place, low)


def owned_kernel(n_edge, edge_ref, asked_ref, near_ref, back_ref, packed_ref, kept_out, sent_out, packed_out, total):
    own_count = near_ref.shape[0]
    rows = own_count // n_edge
    place = onehot(asked_ref[...], (own_count, asked_ref.shape[1]), 0)
    total[...] = near_ref[...] + dot(place, back_ref[...])
    edge = edge_ref[0]
    for j in range(n_edge // 2):
        mask = ring_mask(j)
        owner = edge ^ (2 * mask)
        for out, who in ((kept_out, owner), (sent_out, owner ^ 1)):
            out[j] = total[pl.ds(pl.multiple_of(who * rows, 8), rows), :]


def add_kernel(kept_ref, got_ref, kept_out, sent_out):
    half = kept_out.shape[0]
    kept_out[...] = kept_ref[:half] + got_ref[:half].astype(F32)
    sent_out[...] = (kept_ref[half:] + got_ref[half:].astype(F32)).astype(BF)


def last_kernel(kept_ref, got_ref, out_ref):
    out_ref[...] = kept_ref[0] + got_ref[0].astype(F32)


def widen(packed, rows):
    values = packed.astype(F32)
    return jnp.concatenate([values[:rows], values[rows : rows + 8] + values[rows + 8 :]], axis=0)


def chip_kernel(rows, kept_ref, got_ref, own_out, *packs):
    own_out[...] = kept_ref[0] + widen(got_ref[0], rows)
    for j, out in enumerate(packs):
        high, low = halves(kept_ref[j + 1] + widen(got_ref[j + 1], rows))
        out[: rows + 8] = high
        out[rows + 8 :] = low[rows:]


def total_kernel(parts, n_second, *refs):
    own_ref, gots, out_ref = refs[0], refs[1:-2], refs[-1]
    share = own_ref.shape[1] // parts
    rows = own_ref.shape[0] - 8
    lanes = out_ref.shape[1]
    total = own_ref[...]
    for ref in gots:
        total = total + widen(ref[...], rows)
    hidden = total.shape[1]
    turned = jnp.concatenate([total[:rows], jnp.zeros((lanes - rows, hidden), F32)], axis=0).T
    third = total[rows : rows + 1, :n_second]
    loss = total[rows + 1 : rows + 2, :1]
    mine = lax.broadcasted_iota(I32, (hidden, n_second), 0) % share
    mine = mine == lax.broadcasted_iota(I32, (hidden, n_second), 1) % share
    lane = lax.broadcasted_iota(I32, (n_second, lanes), 1) - rows
    group = lax.broadcasted_iota(I32, (n_second, lanes), 0) // share
    groups = n_second // share
    for part, values in enumerate(halves(third)):
        spread = jnp.where(mine, jnp.broadcast_to(values.astype(F32), (hidden, n_second)), 0.0)
        turned = turned + dot(
            spread.astype(BF), jnp.where(lane == group + part * groups, 1.0, 0.0).astype(BF)
        )
    lane = lax.broadcasted_iota(I32, (hidden, lanes), 1) - rows - 2 * groups
    for part, values in enumerate(halves(loss)):
        turned = turned + jnp.where(lane == part, values.astype(F32), 0.0)
    out_ref[...] = turned.astype(BF)


def final_kernel(rows1, rows2, got_ref, first_out, second_out, third_out, loss_out):
    total = jnp.sum(got_ref[...].astype(F32), axis=0)
    share, lanes = total.shape
    rows = rows1 + rows2
    n_second = third_out.shape[1]
    groups = n_second // share
    first_out[...] = total[:, :rows1]
    second_out[...] = total[:, rows1:rows]
    lane = lax.broadcasted_iota(I32, (lanes, n_second), 0) - rows
    group = lax.broadcasted_iota(I32, (lanes, n_second), 1) // share
    take = jnp.where((lane == group) | (lane == group + groups), 1.0, 0.0)
    spread = lax.dot_general(
        total, take, (((1,), (0,)), ((), ())),
        precision=lax.Precision.HIGHEST, preferred_element_type=F32,
    )
    mine = lax.broadcasted_iota(I32, (share, n_second), 0)
    mine = mine == lax.broadcasted_iota(I32, (share, n_second), 1) % share
    third_out[...] = jnp.sum(jnp.where(mine, spread, 0.0), axis=0, keepdims=True)
    place = rows + 2 * groups
    loss_out[...] = total[0:1, place : place + 1] + total[0:1, place + 1 : place + 2]


def body(node_rows, w_first, w_second, w_third, src_row, requests, slot_index, labels, live_count):
    own_count, width = node_rows.shape
    edges = src_row.shape[0]
    parts, cap = requests.shape
    n_edge = lax.axis_size("edge")
    chips = n_edge // 2
    slots = parts * cap
    hidden, hidden2 = w_second.shape
    scale = 1.0 / math.sqrt(edges * parts * n_edge)
    edge = lax.axis_index("edge").astype(I32).reshape(1)
    sibling = [(i, i ^ 1) for i in range(n_edge)]

    def ahead(step):
        return [(i, (i + 2 * step) % n_edge) for i in range(n_edge)]

    steps = tuple(range(2, chips - 1)) + (1, chips - 1)
    rows1 = 3 * width // n_edge
    rows2 = hidden2 // n_edge
    rows = rows1 + rows2
    cols = jnp.stack([src_row, slot_index, labels], axis=1)
    lines = jnp.stack([src_row, slot_index], axis=0)

    asked_here = lax.all_to_all(requests, "dom", split_axis=0, concat_axis=0, tiled=True)
    answer, asked_line = pl.pallas_call(
        answer_kernel,
        out_shape=(
            jax.ShapeDtypeStruct((slots, width), BF),
            jax.ShapeDtypeStruct((1, slots), I32),
        ),
        in_specs=[WHOLE, FAR],
        out_specs=(WHOLE, WHOLE),
        scratch_shapes=[pltpu.VMEM((own_count, width), BF), pltpu.SemaphoreType.DMA],
        compiler_params=params(8),
        name="answer",
    )(asked_here, in_hbm(node_rows))
    replies = lax.all_to_all(
        answer.reshape(parts, cap, width), "dom", split_axis=0, concat_axis=0, tiled=True
    ).reshape(slots, width)

    outs = [(slots, width), (edges, hidden), (edges, hidden), (edges, hidden2)]
    slot_grad, first, back_first, back_second, extra = pl.pallas_call(
        functools.partial(pair_kernel, scale),
        out_shape=tuple(pltpu.HBM(shape, BF) for shape in outs)
        + (jax.ShapeDtypeStruct((8, hidden), F32),),
        in_specs=[SCALARS] + [WHOLE] * 4 + [FAR] + [WHOLE] * 2,
        out_specs=(FAR,) * 4 + (WHOLE,),
        scratch_shapes=[pltpu.VMEM((3 * width, hidden), BF)]
        + [pltpu.VMEM(shape, BF) for shape in outs]
        + [pltpu.SemaphoreType.DMA((3,)), pltpu.SemaphoreType.DMA((3 * edges // TILE + 1,))],
        compiler_params=params(32),
        cost_estimate=cost(6 * 10**9, 8 * MIB),
        name="pair",
    )(
        live_count, cols, slot_index.reshape(1, edges), node_rows, replies, in_hbm(w_first), w_second,
        w_third.reshape(1, hidden2),
    )

    returned = lax.all_to_all(
        slot_grad.reshape(parts, cap, width), "dom", split_axis=0, concat_axis=0, tiled=True
    ).reshape(slots, width)

    kept, sent = pl.pallas_call(
        functools.partial(weight_kernel, scale, n_edge),
        out_shape=(
            jax.ShapeDtypeStruct((chips, rows + 8, hidden), F32),
            jax.ShapeDtypeStruct((chips, rows + 16, hidden), BF),
        ),
        in_specs=[SCALARS, WHOLE] + [FAR] * 5 + [WHOLE],
        out_specs=(WHOLE, WHOLE),
        scratch_shapes=[
            pltpu.VMEM((3 * width, hidden), F32),
            pltpu.VMEM((hidden2, hidden), F32),
            pltpu.VMEM((own_count, width), BF),
            pltpu.VMEM((slots, width), BF),
            pltpu.VMEM((edges, hidden), BF),
            pltpu.VMEM((edges, hidden), BF),
            pltpu.VMEM((edges, hidden2), BF),
            pltpu.SemaphoreType.DMA((5,)),
        ],
        compiler_params=params(32),
        cost_estimate=FREE,
        name="weights",
    )(
        edge, lines, in_hbm(node_rows), in_hbm(replies), in_hbm(first), in_hbm(back_first),
        in_hbm(back_second), extra,
    )
    near_part = pl.pallas_call(
        near_kernel,
        out_shape=jax.ShapeDtypeStruct((own_count, width), F32),
        in_specs=[WHOLE] * 5,
        out_specs=WHOLE,
        compiler_params=params(32),
        cost_estimate=FREE,
        name="near",
    )(lines, cols, replies, back_first, w_first)

    pack = jax.ShapeDtypeStruct((rows + 16, hidden), BF)
    own, *packs = pl.pallas_call(
        functools.partial(chip_kernel, rows),
        out_shape=(jax.ShapeDtypeStruct((rows + 8, hidden), F32),) + (pack,) * (chips - 1),
        in_specs=[WHOLE] * 2,
        out_specs=(WHOLE,) * chips,
        compiler_params=params(16),
        cost_estimate=FREE,
        name="chip",
    )(kept, lax.ppermute(sent, "edge", sibling))
    gots = [lax.ppermute(packs[step - 1], "edge", ahead(step)) for step in steps]

    share = hidden // parts
    lanes = -(-(rows + 2 * (hidden2 // share) + 2) // 128) * 128
    packed = pl.pallas_call(
        functools.partial(total_kernel, parts, hidden2),
        out_shape=jax.ShapeDtypeStruct((hidden, lanes), BF),
        in_specs=[WHOLE] * chips + [ANYWHERE],
        out_specs=WHOLE,
        compiler_params=params(16),
        cost_estimate=FREE,
        name="total",
    )(own, *gots, near_part)
    block = jax.ShapeDtypeStruct((chips, own_count // n_edge, width), F32)
    kept, sent, packed = pl.pallas_call(
        functools.partial(owned_kernel, n_edge),
        out_shape=(block, block, jax.ShapeDtypeStruct(packed.shape, BF)),
        in_specs=[SCALARS] + [WHOLE] * 3 + [ANYWHERE],
        out_specs=(WHOLE, WHOLE, ANYWHERE),
        input_output_aliases={4: 2},
        scratch_shapes=[pltpu.VMEM((own_count, width), F32)],
        compiler_params=params(8),
        cost_estimate=FREE,
        name="owned",
    )(edge, asked_line, near_part, returned, packed)
    got = lax.all_to_all(
        packed.reshape(parts, share, lanes), "dom", split_axis=0, concat_axis=0, tiled=True
    )
    first_t, second_share, third_total, loss_total = pl.pallas_call(
        functools.partial(final_kernel, rows1, rows2),
        out_shape=(
            jax.ShapeDtypeStruct((share, rows1), F32),
            jax.ShapeDtypeStruct((share, rows2), F32),
            jax.ShapeDtypeStruct((1, hidden2), F32),
            jax.ShapeDtypeStruct((1, 1), F32),
        ),
        in_specs=[WHOLE],
        out_specs=(WHOLE,) * 4,
        compiler_params=params(8),
        cost_estimate=FREE,
        name="final",
    )(got)

    for mask in (0, 1, 3):
        partner = sibling if mask == 0 else [(i, i ^ (2 * mask)) for i in range(n_edge)]
        got = lax.ppermute(sent, "edge", partner)
        if mask == 3:
            break
        half = (kept.shape[0] // 2,) + kept.shape[1:]
        kept, sent = pl.pallas_call(
            add_kernel,
            out_shape=(jax.ShapeDtypeStruct(half, F32), jax.ShapeDtypeStruct(half, BF)),
            in_specs=[WHOLE] * 2,
            out_specs=(WHOLE,) * 2,
            compiler_params=params(8),
            cost_estimate=FREE,
            name="add",
        )(kept, got)
    node_share = pl.pallas_call(
        last_kernel,
        out_shape=jax.ShapeDtypeStruct(kept.shape[1:], F32),
        in_specs=[WHOLE] * 2,
        out_specs=WHOLE,
        compiler_params=params(8),
        cost_estimate=cost(LAST, 0),
        name="last",
    )(kept, got)
    return (
        first_t.T, second_share, third_total.reshape(hidden2), loss_total.reshape(()), node_share
    )


def solution(mesh):
    in_specs = (
        P("dom", None),
        P(),
        P(),
        P(),
        P(("dom", "edge")),
        P(("dom", "edge"), None),
        P(("dom", "edge")),
        P(("dom", "edge")),
        P(("dom", "edge")),
    )
    out_specs = (P("edge", "dom"), P("dom", "edge"), P(), P(), P(("dom", "edge"), None))
    return jax.shard_map(body, mesh=mesh, in_specs=in_specs, out_specs=out_specs, check_vma=False)
```

```python
import functools
import math

import jax
import jax.numpy as jnp
from jax import lax
from jax.experimental import pallas as pl
from jax.experimental.pallas import tpu as pltpu
from jax.sharding import PartitionSpec as P

BF = jnp.bfloat16
F32 = jnp.float32
I32 = jnp.int32
MIB = 1 << 20
TILE = 1024
LAST = 0
WHOLE = pl.BlockSpec(memory_space=pltpu.VMEM)
FREE = pl.CostEstimate(flops=0, bytes_accessed=0, transcendentals=0)
ANYWHERE = pl.BlockSpec(memory_space=pl.ANY)
FAR = pl.BlockSpec(memory_space=pltpu.HBM)
SCALARS = pl.BlockSpec(memory_space=pltpu.SMEM)


def dot(left, right, left_dim=1, right_dim=0):
    return lax.dot_general(
        left, right, (((left_dim,), (right_dim,)), ((), ())), preferred_element_type=F32
    )


def halves(values):
    high = values.astype(BF)
    return high, (values - high.astype(F32)).astype(BF)


def ring_mask(j):
    return (0, 3, 1, 2)[j]


def onehot(index, shape, axis):
    return jnp.where(index == lax.broadcasted_iota(I32, shape, axis), 1.0, 0.0).astype(BF)


def params(mib):
    return pltpu.CompilerParams(vmem_limit_bytes=mib * MIB)


def in_hbm(array):
    return pltpu.with_memory_space_constraint(array, pltpu.HBM)


def cost(flops, nbytes):
    return pl.CostEstimate(flops=flops, bytes_accessed=nbytes, transcendentals=0)


def answer_kernel(asked_ref, node_any, out_ref, line_out, node_ref, sem):
    fetch = pltpu.make_async_copy(node_any, node_ref, sem)
    fetch.start()
    parts, cap = asked_ref.shape
    own_count, slots = node_ref.shape[0], line_out.shape[1]
    spread = lax.broadcasted_iota(I32, (parts, slots), 0)
    spread = spread == lax.broadcasted_iota(I32, (parts, slots), 1) // cap
    lines = dot(asked_ref[...].astype(F32).astype(BF), jnp.where(spread, 1.0, 0.0).astype(BF), 0, 0)
    mine = lax.broadcasted_iota(I32, (cap, slots), 0)
    mine = mine == lax.broadcasted_iota(I32, (cap, slots), 1) % cap
    line = jnp.sum(jnp.where(mine, lines, 0.0), axis=0, keepdims=True).astype(I32)
    line_out[...] = line
    pick = onehot(line, (own_count, slots), 0)
    fetch.wait()
    out_ref[...] = dot(pick, node_ref[...], 0, 0).astype(BF)


def pair_kernel(
    scale, n_edge, live_ref, edge_ref, cols_ref, lines_ref, node_ref, rep_ref, wf_any, ws_ref, wt_ref,
    slot_out, bfirst_out, kept_out, sent_out,
    wf_ref, slot_ref, first_ref, bfirst_ref, bsecond_ref, grads, grads2, extra_ref, sent_ref,
    feat_ref, fetch_sems, store_sems,
):
    edges = cols_ref.shape[0]
    own_count, width = node_ref.shape
    slots = rep_ref.shape[0]
    hidden2 = ws_ref.shape[1]
    fetch = []
    for i in range(3):
        part = pl.ds(i * width, width)
        fetch.append(pltpu.make_async_copy(wf_any.at[part], wf_ref.at[part], fetch_sems.at[i]))
        fetch[-1].start()
    stores = []

    def store(src, dst):
        copy = pltpu.make_async_copy(src, dst, store_sems.at[len(stores)])
        copy.start()
        stores.append(copy)

    w_third = wt_ref[...].astype(F32)
    third = None
    loss = None
    for tile in range(edges // TILE):
        part = pl.ds(tile * TILE, TILE)
        near = dot(onehot(cols_ref[part, 0:1], (TILE, own_count), 1), node_ref[...])
        far = dot(onehot(cols_ref[part, 1:2], (TILE, slots), 1), rep_ref[...])
        target = cols_ref[part, 2:3].astype(F32)
        blocks = (near.astype(BF), far.astype(BF), (near * far).astype(BF))
        pre_first = None
        for i, block in enumerate(blocks):
            feat_ref[i, part] = block
            if tile == 0:
                fetch[i].wait()
            term = dot(block, wf_ref[i * width : (i + 1) * width])
            pre_first = term if pre_first is None else pre_first + term
        sig = jax.nn.sigmoid(pre_first)
        first = (pre_first * sig).astype(BF)
        slope_first = sig * (1.0 + pre_first * (1.0 - sig))
        first_ref[part] = first
        pre_second = dot(first, ws_ref[...])
        sig = jax.nn.sigmoid(pre_second)
        second = (pre_second * sig).astype(BF).astype(F32)
        slope_second = sig * (1.0 + pre_second * (1.0 - sig))
        logits = jnp.sum(second * w_third, axis=1, keepdims=True)
        place = tile * TILE + lax.broadcasted_iota(I32, (TILE, 1), 0)
        live = jnp.where(place < live_ref[0], 1.0, 0.0)
        slope = live * (jax.nn.sigmoid(logits) - target)
        back_second = (slope * w_third * slope_second).astype(BF)
        bsecond_ref[part] = back_second
        back_first = (dot(back_second, ws_ref[...], 1, 1) * slope_first).astype(BF)
        bfirst_ref[part] = back_first
        store(bfirst_ref.at[part], bfirst_out.at[part])
        softplus = jnp.maximum(logits, 0.0) + jnp.log1p(jnp.exp(-jnp.abs(logits)))
        term = jnp.sum(live * (softplus - target * logits), axis=0, keepdims=True)
        loss = term if loss is None else loss + term
        term = jnp.sum(slope * second, axis=0, keepdims=True)
        third = term if third is None else third + term
    extra_ref[...] = jnp.zeros_like(extra_ref)
    extra_ref[0:1, :hidden2] = scale * third
    extra_ref[1:2, :hidden2] = jnp.broadcast_to(scale * loss, (1, hidden2))

    rows1 = 3 * width // n_edge
    rows2 = hidden2 // n_edge
    rows = rows1 + rows2
    bfirst = bfirst_ref[...]
    grads2[...] = scale * dot(bsecond_ref[...], first_ref[...], 0, 0)
    for i in range(3):
        grads[i * width : (i + 1) * width] = scale * dot(feat_ref[i], bfirst, 0, 0)
    edge = edge_ref[0]
    chip = edge // 2
    core = edge % 2
    chips = n_edge // 2
    extra = extra_ref[...]
    extra_high, extra_low = halves(extra)
    for j in range(chips):
        there = 2 * ((chip + j) % chips)
        part1 = pl.ds(pl.multiple_of((there + core) * rows1, 8), rows1)
        part2 = pl.ds(pl.multiple_of((there + core) * rows2, 8), rows2)
        store(grads.at[part1], kept_out.at[j, pl.ds(0, rows1)])
        store(grads2.at[part2], kept_out.at[j, pl.ds(rows1, rows2)])
        store(extra_ref, kept_out.at[j, pl.ds(rows, 8)])
        part1 = pl.ds(pl.multiple_of((there + 1 - core) * rows1, 8), rows1)
        part2 = pl.ds(pl.multiple_of((there + 1 - core) * rows2, 8), rows2)
        sent_ref[j, :rows1] = grads[part1, :].astype(BF)
        sent_ref[j, rows1:rows] = grads2[part2, :].astype(BF)
        sent_ref[j, rows:] = jnp.concatenate([extra_high, extra_low], axis=0)
        store(sent_ref.at[j], sent_out.at[j])

    total = None
    for tile in range(edges // TILE):
        part = pl.ds(tile * TILE, TILE)
        back_first = bfirst_ref[part]
        block_b = dot(back_first, wf_ref[width : 2 * width], 1, 1)
        block_c = dot(back_first, wf_ref[2 * width :], 1, 1)
        high, low = halves(block_b + block_c * feat_ref[0, part].astype(F32))
        place = onehot(lines_ref[1:2, part], (slots, TILE), 0)
        term = dot(place, high) + dot(place, low)
        total = term if total is None else total + term
    slot_ref[...] = total.astype(BF)
    store(slot_ref, slot_out)
    for copy in stores:
        copy.wait()


def near_kernel(lines_ref, cols_ref, rep_ref, bfirst_ref, wf_ref, out_ref):
    edges = lines_ref.shape[1]
    slots, width = rep_ref.shape
    bfirst = bfirst_ref[...]
    far = dot(onehot(cols_ref[:, 1:2], (edges, slots), 1), rep_ref[...])
    block_a = dot(bfirst, wf_ref[:width], 1, 1)
    block_c = dot(bfirst, wf_ref[2 * width :], 1, 1)
    high, low = halves(block_a + block_c * far)
    place = onehot(lines_ref[0:1, :], (out_ref.shape[0], edges), 0)
    out_ref[...] = dot(place, high) + dot(place, low)


def owned_kernel(n_edge, edge_ref, asked_ref, near_ref, back_ref, packed_ref, kept_out, sent_out, packed_out, total):
    own_count = near_ref.shape[0]
    rows = own_count // n_edge
    place = onehot(asked_ref[...], (own_count, asked_ref.shape[1]), 0)
    total[...] = near_ref[...] + dot(place, back_ref[...])
    edge = edge_ref[0]
    for j in range(n_edge // 2):
        mask = ring_mask(j)
        owner = edge ^ (2 * mask)
        for out, who in ((kept_out, owner), (sent_out, owner ^ 1)):
            out[j] = total[pl.ds(pl.multiple_of(who * rows, 8), rows), :]


def add_kernel(kept_ref, got_ref, kept_out, sent_out):
    half = kept_out.shape[0]
    kept_out[...] = kept_ref[:half] + got_ref[:half].astype(F32)
    sent_out[...] = (kept_ref[half:] + got_ref[half:].astype(F32)).astype(BF)


def last_kernel(kept_ref, got_ref, out_ref):
    out_ref[...] = kept_ref[0] + got_ref[0].astype(F32)


def widen(packed, rows):
    values = packed.astype(F32)
    return jnp.concatenate([values[:rows], values[rows : rows + 8] + values[rows + 8 :]], axis=0)


def chip_kernel(rows, kept_ref, got_ref, own_out, *packs):
    own_out[...] = kept_ref[0] + widen(got_ref[0], rows)
    for j, out in enumerate(packs):
        high, low = halves(kept_ref[j + 1] + widen(got_ref[j + 1], rows))
        out[: rows + 8] = high
        out[rows + 8 :] = low[rows:]


def total_kernel(parts, n_second, *refs):
    own_ref, gots, out_ref = refs[0], refs[1:-2], refs[-1]
    share = own_ref.shape[1] // parts
    rows = own_ref.shape[0] - 8
    lanes = out_ref.shape[1]
    total = own_ref[...]
    for ref in gots:
        total = total + widen(ref[...], rows)
    hidden = total.shape[1]
    turned = jnp.concatenate([total[:rows], jnp.zeros((lanes - rows, hidden), F32)], axis=0).T
    third = total[rows : rows + 1, :n_second]
    loss = total[rows + 1 : rows + 2, :1]
    mine = lax.broadcasted_iota(I32, (hidden, n_second), 0) % share
    mine = mine == lax.broadcasted_iota(I32, (hidden, n_second), 1) % share
    lane = lax.broadcasted_iota(I32, (n_second, lanes), 1) - rows
    group = lax.broadcasted_iota(I32, (n_second, lanes), 0) // share
    groups = n_second // share
    for part, values in enumerate(halves(third)):
        spread = jnp.where(mine, jnp.broadcast_to(values.astype(F32), (hidden, n_second)), 0.0)
        turned = turned + dot(
            spread.astype(BF), jnp.where(lane == group + part * groups, 1.0, 0.0).astype(BF)
        )
    lane = lax.broadcasted_iota(I32, (hidden, lanes), 1) - rows - 2 * groups
    for part, values in enumerate(halves(loss)):
        turned = turned + jnp.where(lane == part, values.astype(F32), 0.0)
    out_ref[...] = turned.astype(BF)


def final_kernel(rows1, rows2, got_ref, first_out, second_out, third_out, loss_out):
    total = jnp.sum(got_ref[...].astype(F32), axis=0)
    share, lanes = total.shape
    rows = rows1 + rows2
    n_second = third_out.shape[1]
    groups = n_second // share
    first_out[...] = total[:, :rows1]
    second_out[...] = total[:, rows1:rows]
    lane = lax.broadcasted_iota(I32, (lanes, n_second), 0) - rows
    group = lax.broadcasted_iota(I32, (lanes, n_second), 1) // share
    take = jnp.where((lane == group) | (lane == group + groups), 1.0, 0.0)
    spread = lax.dot_general(
        total, take, (((1,), (0,)), ((), ())),
        precision=lax.Precision.HIGHEST, preferred_element_type=F32,
    )
    mine = lax.broadcasted_iota(I32, (share, n_second), 0)
    mine = mine == lax.broadcasted_iota(I32, (share, n_second), 1) % share
    third_out[...] = jnp.sum(jnp.where(mine, spread, 0.0), axis=0, keepdims=True)
    place = rows + 2 * groups
    loss_out[...] = total[0:1, place : place + 1] + total[0:1, place + 1 : place + 2]


def body(node_rows, w_first, w_second, w_third, src_row, requests, slot_index, labels, live_count):
    own_count, width = node_rows.shape
    edges = src_row.shape[0]
    parts, cap = requests.shape
    n_edge = lax.axis_size("edge")
    chips = n_edge // 2
    slots = parts * cap
    hidden, hidden2 = w_second.shape
    scale = 1.0 / math.sqrt(edges * parts * n_edge)
    edge = lax.axis_index("edge").astype(I32).reshape(1)
    sibling = [(i, i ^ 1) for i in range(n_edge)]

    def ahead(step):
        return [(i, (i + 2 * step) % n_edge) for i in range(n_edge)]

    steps = tuple(range(2, chips - 1)) + (1, chips - 1)
    rows1 = 3 * width // n_edge
    rows2 = hidden2 // n_edge
    rows = rows1 + rows2
    cols = jnp.stack([src_row, slot_index, labels], axis=1)
    lines = jnp.stack([src_row, slot_index], axis=0)

    asked_here = lax.all_to_all(requests, "dom", split_axis=0, concat_axis=0, tiled=True)
    answer, asked_line = pl.pallas_call(
        answer_kernel,
        out_shape=(
            jax.ShapeDtypeStruct((slots, width), BF),
            jax.ShapeDtypeStruct((1, slots), I32),
        ),
        in_specs=[WHOLE, FAR],
        out_specs=(WHOLE, WHOLE),
        scratch_shapes=[pltpu.VMEM((own_count, width), BF), pltpu.SemaphoreType.DMA],
        compiler_params=params(8),
        name="answer",
    )(asked_here, in_hbm(node_rows))
    replies = lax.all_to_all(
        answer.reshape(parts, cap, width), "dom", split_axis=0, concat_axis=0, tiled=True
    ).reshape(slots, width)

    outs = [(slots, width), (edges, hidden), (chips, rows + 8, hidden), (chips, rows + 16, hidden)]
    slot_grad, back_first, kept, sent = pl.pallas_call(
        functools.partial(pair_kernel, scale, n_edge),
        out_shape=tuple(pltpu.HBM(shape, dtype) for shape, dtype in zip(outs, (BF, BF, F32, BF))),
        in_specs=[SCALARS] * 2 + [WHOLE] * 4 + [FAR] + [WHOLE] * 2,
        out_specs=(FAR,) * 4,
        scratch_shapes=[
            pltpu.VMEM((3 * width, hidden), BF),
            pltpu.VMEM((slots, width), BF),
            pltpu.VMEM((edges, hidden), BF),
            pltpu.VMEM((edges, hidden), BF),
            pltpu.VMEM((edges, hidden2), BF),
            pltpu.VMEM((3 * width, hidden), F32),
            pltpu.VMEM((hidden2, hidden), F32),
            pltpu.VMEM((8, hidden), F32),
            pltpu.VMEM((chips, rows + 16, hidden), BF),
            pltpu.VMEM((3, edges, width), BF),
            pltpu.SemaphoreType.DMA((3,)),
            pltpu.SemaphoreType.DMA((edges // TILE + 1 + 4 * chips,)),
        ],
        compiler_params=params(48),
        cost_estimate=cost(6 * 10**9, 8 * MIB),
        name="pair",
    )(live_count, edge, cols, lines, node_rows, replies, in_hbm(w_first), w_second, w_third.reshape(1, hidden2))

    returned = lax.all_to_all(
        slot_grad.reshape(parts, cap, width), "dom", split_axis=0, concat_axis=0, tiled=True
    ).reshape(slots, width)

    near_part = pl.pallas_call(
        near_kernel,
        out_shape=jax.ShapeDtypeStruct((own_count, width), F32),
        in_specs=[WHOLE] * 5,
        out_specs=WHOLE,
        compiler_params=params(32),
        cost_estimate=FREE,
        name="near",
    )(lines, cols, replies, back_first, w_first)

    pack = jax.ShapeDtypeStruct((rows + 16, hidden), BF)
    own, *packs = pl.pallas_call(
        functools.partial(chip_kernel, rows),
        out_shape=(jax.ShapeDtypeStruct((rows + 8, hidden), F32),) + (pack,) * (chips - 1),
        in_specs=[WHOLE] * 2,
        out_specs=(WHOLE,) * chips,
        compiler_params=params(16),
        cost_estimate=FREE,
        name="chip",
    )(kept, lax.ppermute(sent, "edge", sibling))
    gots = [lax.ppermute(packs[step - 1], "edge", ahead(step)) for step in steps]

    share = hidden // parts
    lanes = -(-(rows + 2 * (hidden2 // share) + 2) // 128) * 128
    packed = pl.pallas_call(
        functools.partial(total_kernel, parts, hidden2),
        out_shape=jax.ShapeDtypeStruct((hidden, lanes), BF),
        in_specs=[WHOLE] * chips + [ANYWHERE],
        out_specs=WHOLE,
        compiler_params=params(16),
        cost_estimate=FREE,
        name="total",
    )(own, *gots, near_part)
    block = jax.ShapeDtypeStruct((chips, own_count // n_edge, width), F32)
    kept, sent, packed = pl.pallas_call(
        functools.partial(owned_kernel, n_edge),
        out_shape=(block, block, jax.ShapeDtypeStruct(packed.shape, BF)),
        in_specs=[SCALARS] + [WHOLE] * 3 + [ANYWHERE],
        out_specs=(WHOLE, WHOLE, ANYWHERE),
        input_output_aliases={4: 2},
        scratch_shapes=[pltpu.VMEM((own_count, width), F32)],
        compiler_params=params(8),
        cost_estimate=FREE,
        name="owned",
    )(edge, asked_line, near_part, returned, packed)
    got = lax.all_to_all(
        packed.reshape(parts, share, lanes), "dom", split_axis=0, concat_axis=0, tiled=True
    )
    first_t, second_share, third_total, loss_total = pl.pallas_call(
        functools.partial(final_kernel, rows1, rows2),
        out_shape=(
            jax.ShapeDtypeStruct((share, rows1), F32),
            jax.ShapeDtypeStruct((share, rows2), F32),
            jax.ShapeDtypeStruct((1, hidden2), F32),
            jax.ShapeDtypeStruct((1, 1), F32),
        ),
        in_specs=[WHOLE],
        out_specs=(WHOLE,) * 4,
        compiler_params=params(8),
        cost_estimate=FREE,
        name="final",
    )(got)

    for mask in (0, 1, 3):
        partner = sibling if mask == 0 else [(i, i ^ (2 * mask)) for i in range(n_edge)]
        got = lax.ppermute(sent, "edge", partner)
        if mask == 3:
            break
        half = (kept.shape[0] // 2,) + kept.shape[1:]
        kept, sent = pl.pallas_call(
            add_kernel,
            out_shape=(jax.ShapeDtypeStruct(half, F32), jax.ShapeDtypeStruct(half, BF)),
            in_specs=[WHOLE] * 2,
            out_specs=(WHOLE,) * 2,
            compiler_params=params(8),
            cost_estimate=FREE,
            name="add",
        )(kept, got)
    node_share = pl.pallas_call(
        last_kernel,
        out_shape=jax.ShapeDtypeStruct(kept.shape[1:], F32),
        in_specs=[WHOLE] * 2,
        out_specs=WHOLE,
        compiler_params=params(8),
        cost_estimate=cost(LAST, 0),
        name="last",
    )(kept, got)
    return (
        first_t.T, second_share, third_total.reshape(hidden2), loss_total.reshape(()), node_share
    )


def solution(mesh):
    in_specs = (
        P("dom", None),
        P(),
        P(),
        P(),
        P(("dom", "edge")),
        P(("dom", "edge"), None),
        P(("dom", "edge")),
        P(("dom", "edge")),
        P(("dom", "edge")),
    )
    out_specs = (P("edge", "dom"), P("dom", "edge"), P(), P(), P(("dom", "edge"), None))
    return jax.shard_map(body, mesh=mesh, in_specs=in_specs, out_specs=out_specs, check_vma=False)
```

```python
import functools
import math

import jax
import jax.numpy as jnp
from jax import lax
from jax.experimental import pallas as pl
from jax.experimental.pallas import tpu as pltpu
from jax.sharding import PartitionSpec as P

BF = jnp.bfloat16
F32 = jnp.float32
I32 = jnp.int32
MIB = 1 << 20
TILE = 1024
LAST = 0
WHOLE = pl.BlockSpec(memory_space=pltpu.VMEM)
FREE = pl.CostEstimate(flops=0, bytes_accessed=0, transcendentals=0)
ANYWHERE = pl.BlockSpec(memory_space=pl.ANY)
FAR = pl.BlockSpec(memory_space=pltpu.HBM)
SCALARS = pl.BlockSpec(memory_space=pltpu.SMEM)


def dot(left, right, left_dim=1, right_dim=0):
    return lax.dot_general(
        left, right, (((left_dim,), (right_dim,)), ((), ())), preferred_element_type=F32
    )


def halves(values):
    high = values.astype(BF)
    return high, (values - high.astype(F32)).astype(BF)


def ring_mask(j):
    return (0, 3, 1, 2)[j]


def onehot(index, shape, axis):
    return jnp.where(index == lax.broadcasted_iota(I32, shape, axis), 1.0, 0.0).astype(BF)


def params(mib):
    return pltpu.CompilerParams(vmem_limit_bytes=mib * MIB)


def in_hbm(array):
    return pltpu.with_memory_space_constraint(array, pltpu.HBM)


def cost(flops, nbytes):
    return pl.CostEstimate(flops=flops, bytes_accessed=nbytes, transcendentals=0)


def answer_kernel(asked_ref, node_any, out_ref, line_out, node_ref, sem):
    fetch = pltpu.make_async_copy(node_any, node_ref, sem)
    fetch.start()
    parts, cap = asked_ref.shape
    own_count, slots = node_ref.shape[0], line_out.shape[1]
    spread = lax.broadcasted_iota(I32, (parts, slots), 0)
    spread = spread == lax.broadcasted_iota(I32, (parts, slots), 1) // cap
    lines = dot(asked_ref[...].astype(F32).astype(BF), jnp.where(spread, 1.0, 0.0).astype(BF), 0, 0)
    mine = lax.broadcasted_iota(I32, (cap, slots), 0)
    mine = mine == lax.broadcasted_iota(I32, (cap, slots), 1) % cap
    line = jnp.sum(jnp.where(mine, lines, 0.0), axis=0, keepdims=True).astype(I32)
    line_out[...] = line
    pick = onehot(line, (own_count, slots), 0)
    fetch.wait()
    out_ref[...] = dot(pick, node_ref[...], 0, 0).astype(BF)


def pair_kernel(
    scale, n_edge, live_ref, edge_ref, cols_ref, lines_ref, node_ref, rep_ref, wf_any, ws_ref, wt_ref,
    slot_out, bfirst_out, kept_out, sent_out,
    wf_ref, slot_ref, first_ref, bfirst_ref, bsecond_ref, grads, grads2, extra_ref, sent_ref,
    feat_ref, fetch_sems, store_sems,
):
    edges = cols_ref.shape[0]
    own_count, width = node_ref.shape
    slots = rep_ref.shape[0]
    hidden2 = ws_ref.shape[1]
    fetch = []
    for i in range(3):
        part = pl.ds(i * width, width)
        fetch.append(pltpu.make_async_copy(wf_any.at[part], wf_ref.at[part], fetch_sems.at[i]))
        fetch[-1].start()
    stores = []

    def store(src, dst):
        copy = pltpu.make_async_copy(src, dst, store_sems.at[len(stores)])
        copy.start()
        stores.append(copy)

    w_third = wt_ref[...].astype(F32)
    third = None
    loss = None
    for tile in range(edges // TILE):
        part = pl.ds(tile * TILE, TILE)
        near = dot(onehot(cols_ref[part, 0:1], (TILE, own_count), 1), node_ref[...])
        far = dot(onehot(cols_ref[part, 1:2], (TILE, slots), 1), rep_ref[...])
        target = cols_ref[part, 2:3].astype(F32)
        blocks = (near.astype(BF), far.astype(BF), (near * far).astype(BF))
        pre_first = None
        for i, block in enumerate(blocks):
            feat_ref[i, part] = block
            if tile == 0:
                fetch[i].wait()
            term = dot(block, wf_ref[i * width : (i + 1) * width])
            pre_first = term if pre_first is None else pre_first + term
        sig = jax.nn.sigmoid(pre_first)
        first = (pre_first * sig).astype(BF)
        slope_first = sig * (1.0 + pre_first * (1.0 - sig))
        first_ref[part] = first
        pre_second = dot(first, ws_ref[...])
        sig = jax.nn.sigmoid(pre_second)
        second_b = (pre_second * sig).astype(BF)
        second = second_b.astype(F32)
        slope_second = sig * (1.0 + pre_second * (1.0 - sig))
        logits = dot(second_b, jnp.broadcast_to(wt_ref[...], (hidden2, hidden2)), 1, 1)
        place = tile * TILE + lax.broadcasted_iota(I32, (TILE, hidden2), 0)
        live = jnp.where(place < live_ref[0], 1.0, 0.0)
        slope = live * (jax.nn.sigmoid(logits) - target)
        back_second = (slope * w_third * slope_second).astype(BF)
        bsecond_ref[part] = back_second
        back_first = (dot(back_second, ws_ref[...], 1, 1) * slope_first).astype(BF)
        bfirst_ref[part] = back_first
        store(bfirst_ref.at[part], bfirst_out.at[part])
        softplus = jnp.maximum(logits, 0.0) + jnp.log1p(jnp.exp(-jnp.abs(logits)))
        term = jnp.sum(live * (softplus - target * logits), axis=0, keepdims=True)
        loss = term if loss is None else loss + term
        term = jnp.sum(slope * second, axis=0, keepdims=True)
        third = term if third is None else third + term
    extra_ref[...] = jnp.zeros_like(extra_ref)
    extra_ref[0:1, :hidden2] = scale * third
    extra_ref[1:2, :hidden2] = scale * loss

    rows1 = 3 * width // n_edge
    rows2 = hidden2 // n_edge
    rows = rows1 + rows2
    bfirst = bfirst_ref[...]
    grads2[...] = scale * dot(bsecond_ref[...], first_ref[...], 0, 0)
    for i in range(3):
        grads[i * width : (i + 1) * width] = scale * dot(feat_ref[i], bfirst, 0, 0)
    edge = edge_ref[0]
    chip = edge // 2
    core = edge % 2
    chips = n_edge // 2
    extra = extra_ref[...]
    extra_high, extra_low = halves(extra)
    for j in range(chips):
        there = 2 * ((chip + j) % chips)
        part1 = pl.ds(pl.multiple_of((there + core) * rows1, 8), rows1)
        part2 = pl.ds(pl.multiple_of((there + core) * rows2, 8), rows2)
        store(grads.at[part1], kept_out.at[j, pl.ds(0, rows1)])
        store(grads2.at[part2], kept_out.at[j, pl.ds(rows1, rows2)])
        store(extra_ref, kept_out.at[j, pl.ds(rows, 8)])
        part1 = pl.ds(pl.multiple_of((there + 1 - core) * rows1, 8), rows1)
        part2 = pl.ds(pl.multiple_of((there + 1 - core) * rows2, 8), rows2)
        sent_ref[j, :rows1] = grads[part1, :].astype(BF)
        sent_ref[j, rows1:rows] = grads2[part2, :].astype(BF)
        sent_ref[j, rows:] = jnp.concatenate([extra_high, extra_low], axis=0)
        store(sent_ref.at[j], sent_out.at[j])

    total = None
    for tile in range(edges // TILE):
        part = pl.ds(tile * TILE, TILE)
        back_first = bfirst_ref[part]
        block_b = dot(back_first, wf_ref[width : 2 * width], 1, 1)
        block_c = dot(back_first, wf_ref[2 * width :], 1, 1)
        place = onehot(lines_ref[1:2, part], (slots, TILE), 0)
        term = dot(place, (block_b + block_c * feat_ref[0, part].astype(F32)).astype(BF))
        total = term if total is None else total + term
    slot_ref[...] = total.astype(BF)
    store(slot_ref, slot_out)
    for copy in stores:
        copy.wait()


def near_kernel(lines_ref, cols_ref, rep_ref, bfirst_ref, wf_ref, out_ref):
    edges = lines_ref.shape[1]
    slots, width = rep_ref.shape
    bfirst = bfirst_ref[...]
    far = dot(onehot(cols_ref[:, 1:2], (edges, slots), 1), rep_ref[...])
    block_a = dot(bfirst, wf_ref[:width], 1, 1)
    block_c = dot(bfirst, wf_ref[2 * width :], 1, 1)
    high, low = halves(block_a + block_c * far)
    place = onehot(lines_ref[0:1, :], (out_ref.shape[0], edges), 0)
    out_ref[...] = dot(place, high) + dot(place, low)


def owned_kernel(n_edge, edge_ref, asked_ref, near_ref, back_ref, packed_ref, kept_out, sent_out, packed_out, total):
    own_count = near_ref.shape[0]
    rows = own_count // n_edge
    place = onehot(asked_ref[...], (own_count, asked_ref.shape[1]), 0)
    total[...] = near_ref[...] + dot(place, back_ref[...])
    edge = edge_ref[0]
    for j in range(n_edge // 2):
        mask = ring_mask(j)
        owner = edge ^ (2 * mask)
        for out, who in ((kept_out, owner), (sent_out, owner ^ 1)):
            out[j] = total[pl.ds(pl.multiple_of(who * rows, 8), rows), :]


def add_kernel(kept_ref, got_ref, kept_out, sent_out):
    half = kept_out.shape[0]
    kept_out[...] = kept_ref[:half] + got_ref[:half].astype(F32)
    sent_out[...] = (kept_ref[half:] + got_ref[half:].astype(F32)).astype(BF)


def last_kernel(kept_ref, got_ref, out_ref):
    out_ref[...] = kept_ref[0] + got_ref[0].astype(F32)


def widen(packed, rows):
    values = packed.astype(F32)
    return jnp.concatenate([values[:rows], values[rows : rows + 8] + values[rows + 8 :]], axis=0)


def chip_kernel(rows, kept_ref, got_ref, own_out, *packs):
    own_out[...] = kept_ref[0] + widen(got_ref[0], rows)
    for j, out in enumerate(packs):
        high, low = halves(kept_ref[j + 1] + widen(got_ref[j + 1], rows))
        out[: rows + 8] = high
        out[rows + 8 :] = low[rows:]


def total_kernel(parts, n_second, *refs):
    own_ref, gots, out_ref = refs[0], refs[1:-2], refs[-1]
    share = own_ref.shape[1] // parts
    rows = own_ref.shape[0] - 8
    lanes = out_ref.shape[1]
    total = own_ref[...]
    for ref in gots:
        total = total + widen(ref[...], rows)
    hidden = total.shape[1]
    turned = jnp.concatenate([total[:rows], jnp.zeros((lanes - rows, hidden), F32)], axis=0).T
    third = total[rows : rows + 1, :n_second]
    loss = total[rows + 1 : rows + 2, :1]
    mine = lax.broadcasted_iota(I32, (hidden, n_second), 0) % share
    mine = mine == lax.broadcasted_iota(I32, (hidden, n_second), 1) % share
    lane = lax.broadcasted_iota(I32, (n_second, lanes), 1) - rows
    group = lax.broadcasted_iota(I32, (n_second, lanes), 0) // share
    groups = n_second // share
    for part, values in enumerate(halves(third)):
        spread = jnp.where(mine, jnp.broadcast_to(values.astype(F32), (hidden, n_second)), 0.0)
        turned = turned + dot(
            spread.astype(BF), jnp.where(lane == group + part * groups, 1.0, 0.0).astype(BF)
        )
    lane = lax.broadcasted_iota(I32, (hidden, lanes), 1) - rows - 2 * groups
    for part, values in enumerate(halves(loss)):
        turned = turned + jnp.where(lane == part, values.astype(F32), 0.0)
    out_ref[...] = turned.astype(BF)


def final_kernel(rows1, rows2, got_ref, first_out, second_out, third_out, loss_out):
    total = jnp.sum(got_ref[...].astype(F32), axis=0)
    share, lanes = total.shape
    rows = rows1 + rows2
    n_second = third_out.shape[1]
    groups = n_second // share
    first_out[...] = total[:, :rows1]
    second_out[...] = total[:, rows1:rows]
    lane = lax.broadcasted_iota(I32, (lanes, n_second), 0) - rows
    group = lax.broadcasted_iota(I32, (lanes, n_second), 1) // share
    take = jnp.where((lane == group) | (lane == group + groups), 1.0, 0.0)
    spread = lax.dot_general(
        total, take, (((1,), (0,)), ((), ())),
        precision=lax.Precision.HIGHEST, preferred_element_type=F32,
    )
    mine = lax.broadcasted_iota(I32, (share, n_second), 0)
    mine = mine == lax.broadcasted_iota(I32, (share, n_second), 1) % share
    third_out[...] = jnp.sum(jnp.where(mine, spread, 0.0), axis=0, keepdims=True)
    place = rows + 2 * groups
    loss_out[...] = total[0:1, place : place + 1] + total[0:1, place + 1 : place + 2]


def body(node_rows, w_first, w_second, w_third, src_row, requests, slot_index, labels, live_count):
    own_count, width = node_rows.shape
    edges = src_row.shape[0]
    parts, cap = requests.shape
    n_edge = lax.axis_size("edge")
    chips = n_edge // 2
    slots = parts * cap
    hidden, hidden2 = w_second.shape
    scale = 1.0 / math.sqrt(edges * parts * n_edge)
    edge = lax.axis_index("edge").astype(I32).reshape(1)
    sibling = [(i, i ^ 1) for i in range(n_edge)]

    def ahead(step):
        return [(i, (i + 2 * step) % n_edge) for i in range(n_edge)]

    steps = tuple(range(2, chips - 1)) + (1, chips - 1)
    rows1 = 3 * width // n_edge
    rows2 = hidden2 // n_edge
    rows = rows1 + rows2
    cols = jnp.stack([src_row, slot_index, labels], axis=1)
    lines = jnp.stack([src_row, slot_index], axis=0)

    asked_here = lax.all_to_all(requests, "dom", split_axis=0, concat_axis=0, tiled=True)
    answer, asked_line = pl.pallas_call(
        answer_kernel,
        out_shape=(
            jax.ShapeDtypeStruct((slots, width), BF),
            jax.ShapeDtypeStruct((1, slots), I32),
        ),
        in_specs=[WHOLE, FAR],
        out_specs=(WHOLE, WHOLE),
        scratch_shapes=[pltpu.VMEM((own_count, width), BF), pltpu.SemaphoreType.DMA],
        compiler_params=params(8),
        name="answer",
    )(asked_here, in_hbm(node_rows))
    replies = lax.all_to_all(
        answer.reshape(parts, cap, width), "dom", split_axis=0, concat_axis=0, tiled=True
    ).reshape(slots, width)

    outs = [(slots, width), (edges, hidden), (chips, rows + 8, hidden), (chips, rows + 16, hidden)]
    slot_grad, back_first, kept, sent = pl.pallas_call(
        functools.partial(pair_kernel, scale, n_edge),
        out_shape=tuple(pltpu.HBM(shape, dtype) for shape, dtype in zip(outs, (BF, BF, F32, BF))),
        in_specs=[SCALARS] * 2 + [WHOLE] * 4 + [FAR] + [WHOLE] * 2,
        out_specs=(FAR,) * 4,
        scratch_shapes=[
            pltpu.VMEM((3 * width, hidden), BF),
            pltpu.VMEM((slots, width), BF),
            pltpu.VMEM((edges, hidden), BF),
            pltpu.VMEM((edges, hidden), BF),
            pltpu.VMEM((edges, hidden2), BF),
            pltpu.VMEM((3 * width, hidden), F32),
            pltpu.VMEM((hidden2, hidden), F32),
            pltpu.VMEM((8, hidden), F32),
            pltpu.VMEM((chips, rows + 16, hidden), BF),
            pltpu.VMEM((3, edges, width), BF),
            pltpu.SemaphoreType.DMA((3,)),
            pltpu.SemaphoreType.DMA((edges // TILE + 1 + 4 * chips,)),
        ],
        compiler_params=params(48),
        cost_estimate=cost(6 * 10**9, 8 * MIB),
        name="pair",
    )(live_count, edge, cols, lines, node_rows, replies, in_hbm(w_first), w_second, w_third.reshape(1, hidden2))

    returned = lax.all_to_all(
        slot_grad.reshape(parts, cap, width), "dom", split_axis=0, concat_axis=0, tiled=True
    ).reshape(slots, width)

    near_part = pl.pallas_call(
        near_kernel,
        out_shape=jax.ShapeDtypeStruct((own_count, width), F32),
        in_specs=[WHOLE] * 5,
        out_specs=WHOLE,
        compiler_params=params(32),
        cost_estimate=FREE,
        name="near",
    )(lines, cols, replies, back_first, w_first)

    pack = jax.ShapeDtypeStruct((rows + 16, hidden), BF)
    own, *packs = pl.pallas_call(
        functools.partial(chip_kernel, rows),
        out_shape=(jax.ShapeDtypeStruct((rows + 8, hidden), F32),) + (pack,) * (chips - 1),
        in_specs=[WHOLE] * 2,
        out_specs=(WHOLE,) * chips,
        compiler_params=params(16),
        cost_estimate=FREE,
        name="chip",
    )(kept, lax.ppermute(sent, "edge", sibling))
    gots = [lax.ppermute(packs[step - 1], "edge", ahead(step)) for step in steps]

    share = hidden // parts
    lanes = -(-(rows + 2 * (hidden2 // share) + 2) // 128) * 128
    packed = pl.pallas_call(
        functools.partial(total_kernel, parts, hidden2),
        out_shape=jax.ShapeDtypeStruct((hidden, lanes), BF),
        in_specs=[WHOLE] * chips + [ANYWHERE],
        out_specs=WHOLE,
        compiler_params=params(16),
        cost_estimate=FREE,
        name="total",
    )(own, *gots, near_part)
    block = jax.ShapeDtypeStruct((chips, own_count // n_edge, width), F32)
    kept, sent, packed = pl.pallas_call(
        functools.partial(owned_kernel, n_edge),
        out_shape=(block, block, jax.ShapeDtypeStruct(packed.shape, BF)),
        in_specs=[SCALARS] + [WHOLE] * 3 + [ANYWHERE],
        out_specs=(WHOLE, WHOLE, ANYWHERE),
        input_output_aliases={4: 2},
        scratch_shapes=[pltpu.VMEM((own_count, width), F32)],
        compiler_params=params(8),
        cost_estimate=FREE,
        name="owned",
    )(edge, asked_line, near_part, returned, packed)
    got = lax.all_to_all(
        packed.reshape(parts, share, lanes), "dom", split_axis=0, concat_axis=0, tiled=True
    )
    first_t, second_share, third_total, loss_total = pl.pallas_call(
        functools.partial(final_kernel, rows1, rows2),
        out_shape=(
            jax.ShapeDtypeStruct((share, rows1), F32),
            jax.ShapeDtypeStruct((share, rows2), F32),
            jax.ShapeDtypeStruct((1, hidden2), F32),
            jax.ShapeDtypeStruct((1, 1), F32),
        ),
        in_specs=[WHOLE],
        out_specs=(WHOLE,) * 4,
        compiler_params=params(8),
        cost_estimate=FREE,
        name="final",
    )(got)

    for mask in (0, 1, 3):
        partner = sibling if mask == 0 else [(i, i ^ (2 * mask)) for i in range(n_edge)]
        got = lax.ppermute(sent, "edge", partner)
        if mask == 3:
            break
        half = (kept.shape[0] // 2,) + kept.shape[1:]
        kept, sent = pl.pallas_call(
            add_kernel,
            out_shape=(jax.ShapeDtypeStruct(half, F32), jax.ShapeDtypeStruct(half, BF)),
            in_specs=[WHOLE] * 2,
            out_specs=(WHOLE,) * 2,
            compiler_params=params(8),
            cost_estimate=FREE,
            name="add",
        )(kept, got)
    node_share = pl.pallas_call(
        last_kernel,
        out_shape=jax.ShapeDtypeStruct(kept.shape[1:], F32),
        in_specs=[WHOLE] * 2,
        out_specs=WHOLE,
        compiler_params=params(8),
        cost_estimate=cost(LAST, 0),
        name="last",
    )(kept, got)
    return (
        first_t.T, second_share, third_total.reshape(hidden2), loss_total.reshape(()), node_share
    )


def solution(mesh):
    in_specs = (
        P("dom", None),
        P(),
        P(),
        P(),
        P(("dom", "edge")),
        P(("dom", "edge"), None),
        P(("dom", "edge")),
        P(("dom", "edge")),
        P(("dom", "edge")),
    )
    out_specs = (P("edge", "dom"), P("dom", "edge"), P(), P(), P(("dom", "edge"), None))
    return jax.shard_map(body, mesh=mesh, in_specs=in_specs, out_specs=out_specs, check_vma=False)
```

```python
import functools
import math

import jax
import jax.numpy as jnp
from jax import lax
from jax.experimental import pallas as pl
from jax.experimental.pallas import tpu as pltpu
from jax.sharding import PartitionSpec as P

BF = jnp.bfloat16
F32 = jnp.float32
I32 = jnp.int32
MIB = 1 << 20
TILE = 1024
LAST = 0
WHOLE = pl.BlockSpec(memory_space=pltpu.VMEM)
FREE = pl.CostEstimate(flops=0, bytes_accessed=0, transcendentals=0)
ANYWHERE = pl.BlockSpec(memory_space=pl.ANY)
FAR = pl.BlockSpec(memory_space=pltpu.HBM)
SCALARS = pl.BlockSpec(memory_space=pltpu.SMEM)


def dot(left, right, left_dim=1, right_dim=0):
    return lax.dot_general(
        left, right, (((left_dim,), (right_dim,)), ((), ())), preferred_element_type=F32
    )


def halves(values):
    high = values.astype(BF)
    return high, (values - high.astype(F32)).astype(BF)


def ring_mask(j):
    return (0, 3, 1, 2)[j]


def onehot(index, shape, axis):
    return jnp.where(index == lax.broadcasted_iota(I32, shape, axis), 1.0, 0.0).astype(BF)


def params(mib):
    return pltpu.CompilerParams(vmem_limit_bytes=mib * MIB)


def in_hbm(array):
    return pltpu.with_memory_space_constraint(array, pltpu.HBM)


def cost(flops, nbytes):
    return pl.CostEstimate(flops=flops, bytes_accessed=nbytes, transcendentals=0)


def answer_kernel(asked_ref, node_any, out_any, line_out, node_ref, out_ref, sems):
    fetch = pltpu.make_async_copy(node_any, node_ref, sems.at[0])
    fetch.start()
    parts, cap = asked_ref.shape
    own_count, slots = node_ref.shape[0], line_out.shape[1]
    spread = lax.broadcasted_iota(I32, (parts, slots), 0)
    spread = spread == lax.broadcasted_iota(I32, (parts, slots), 1) // cap
    lines = dot(asked_ref[...].astype(F32).astype(BF), jnp.where(spread, 1.0, 0.0).astype(BF), 0, 0)
    mine = lax.broadcasted_iota(I32, (cap, slots), 0)
    mine = mine == lax.broadcasted_iota(I32, (cap, slots), 1) % cap
    line = jnp.sum(jnp.where(mine, lines, 0.0), axis=0, keepdims=True).astype(I32)
    line_out[...] = line
    pick = onehot(line, (own_count, slots), 0)
    fetch.wait()
    half = slots // 2
    stores = []
    for h in range(2):
        part = pl.ds(h * half, half)
        out_ref[part] = dot(pick[:, h * half : (h + 1) * half], node_ref[...], 0, 0).astype(BF)
        stores.append(pltpu.make_async_copy(out_ref.at[part], out_any.at[part], sems.at[1 + h]))
        stores[-1].start()
    for copy in stores:
        copy.wait()


def pair_kernel(
    scale, n_edge, live_ref, edge_ref, cols_ref, lines_ref, node_ref, rep_ref, wf_any, ws_ref, wt_ref,
    slot_out, bfirst_out, kept_out, sent_out,
    wf_ref, slot_ref, first_ref, bfirst_ref, bsecond_ref, grads, grads2, extra_ref, sent_ref,
    feat_ref, fetch_sems, store_sems,
):
    edges = cols_ref.shape[0]
    own_count, width = node_ref.shape
    slots = rep_ref.shape[0]
    hidden2 = ws_ref.shape[1]
    fetch = []
    for i in range(3):
        part = pl.ds(i * width, width)
        fetch.append(pltpu.make_async_copy(wf_any.at[part], wf_ref.at[part], fetch_sems.at[i]))
        fetch[-1].start()
    stores = []

    def store(src, dst):
        copy = pltpu.make_async_copy(src, dst, store_sems.at[len(stores)])
        copy.start()
        stores.append(copy)

    w_third = wt_ref[...].astype(F32)
    third = None
    loss = None
    for tile in range(edges // TILE):
        part = pl.ds(tile * TILE, TILE)
        near = dot(onehot(cols_ref[part, 0:1], (TILE, own_count), 1), node_ref[...])
        far = dot(onehot(cols_ref[part, 1:2], (TILE, slots), 1), rep_ref[...])
        target = cols_ref[part, 2:3].astype(F32)
        blocks = (near.astype(BF), far.astype(BF), (near * far).astype(BF))
        pre_first = None
        for i, block in enumerate(blocks):
            feat_ref[i, part] = block
            if tile == 0:
                fetch[i].wait()
            term = dot(block, wf_ref[i * width : (i + 1) * width])
            pre_first = term if pre_first is None else pre_first + term
        sig = jax.nn.sigmoid(pre_first)
        first = (pre_first * sig).astype(BF)
        slope_first = sig * (1.0 + pre_first * (1.0 - sig))
        first_ref[part] = first
        pre_second = dot(first, ws_ref[...])
        sig = jax.nn.sigmoid(pre_second)
        second_b = (pre_second * sig).astype(BF)
        second = second_b.astype(F32)
        slope_second = sig * (1.0 + pre_second * (1.0 - sig))
        logits = dot(second_b, jnp.broadcast_to(wt_ref[...], (hidden2, hidden2)), 1, 1)
        place = tile * TILE + lax.broadcasted_iota(I32, (TILE, hidden2), 0)
        live = jnp.where(place < live_ref[0], 1.0, 0.0)
        slope = live * (jax.nn.sigmoid(logits) - target)
        back_second = (slope * w_third * slope_second).astype(BF)
        bsecond_ref[part] = back_second
        back_first = (dot(back_second, ws_ref[...], 1, 1) * slope_first).astype(BF)
        bfirst_ref[part] = back_first
        store(bfirst_ref.at[part], bfirst_out.at[part])
        softplus = jnp.maximum(logits, 0.0) + jnp.log1p(jnp.exp(-jnp.abs(logits)))
        term = jnp.sum(live * (softplus - target * logits), axis=0, keepdims=True)
        loss = term if loss is None else loss + term
        term = jnp.sum(slope * second, axis=0, keepdims=True)
        third = term if third is None else third + term
    extra_ref[...] = jnp.zeros_like(extra_ref)
    extra_ref[0:1, :hidden2] = scale * third
    extra_ref[1:2, :hidden2] = scale * loss

    rows1 = 3 * width // n_edge
    rows2 = hidden2 // n_edge
    rows = rows1 + rows2
    bfirst = bfirst_ref[...]
    grads2[...] = scale * dot(bsecond_ref[...], first_ref[...], 0, 0)
    for i in range(3):
        grads[i * width : (i + 1) * width] = scale * dot(feat_ref[i], bfirst, 0, 0)
    edge = edge_ref[0]
    chip = edge // 2
    core = edge % 2
    chips = n_edge // 2
    extra = paired(extra_ref[...])
    for j in range(chips):
        there = 2 * ((chip + j) % chips)
        part1 = pl.ds(pl.multiple_of((there + core) * rows1, 8), rows1)
        part2 = pl.ds(pl.multiple_of((there + core) * rows2, 8), rows2)
        store(grads.at[part1], kept_out.at[j, pl.ds(0, rows1)])
        store(grads2.at[part2], kept_out.at[j, pl.ds(rows1, rows2)])
        store(extra_ref, kept_out.at[j, pl.ds(rows, 8)])
        part1 = pl.ds(pl.multiple_of((there + 1 - core) * rows1, 8), rows1)
        part2 = pl.ds(pl.multiple_of((there + 1 - core) * rows2, 8), rows2)
        sent_ref[j, :rows1] = grads[part1, :].astype(BF)
        sent_ref[j, rows1:rows] = grads2[part2, :].astype(BF)
        sent_ref[j, rows:] = extra
        store(sent_ref.at[j], sent_out.at[j])

    total = None
    for tile in range(edges // TILE):
        part = pl.ds(tile * TILE, TILE)
        back_first = bfirst_ref[part]
        block_b = dot(back_first, wf_ref[width : 2 * width], 1, 1)
        block_c = dot(back_first, wf_ref[2 * width :], 1, 1)
        place = onehot(lines_ref[1:2, part], (slots, TILE), 0)
        term = dot(place, (block_b + block_c * feat_ref[0, part].astype(F32)).astype(BF))
        total = term if total is None else total + term
    slot_ref[...] = total.astype(BF)
    store(slot_ref, slot_out)
    for copy in stores:
        copy.wait()


def near_kernel(lines_ref, cols_ref, rep_ref, bfirst_ref, wf_ref, out_ref):
    edges = lines_ref.shape[1]
    slots, width = rep_ref.shape
    bfirst = bfirst_ref[...]
    far = dot(onehot(cols_ref[:, 1:2], (edges, slots), 1), rep_ref[...])
    block_a = dot(bfirst, wf_ref[:width], 1, 1)
    block_c = dot(bfirst, wf_ref[2 * width :], 1, 1)
    high, low = halves(block_a + block_c * far)
    place = onehot(lines_ref[0:1, :], (out_ref.shape[0], edges), 0)
    out_ref[...] = dot(place, high) + dot(place, low)


def owned_kernel(n_edge, edge_ref, asked_ref, near_ref, back_ref, packed_ref, kept_out, sent_out, packed_out, total):
    own_count = near_ref.shape[0]
    rows = own_count // n_edge
    place = onehot(asked_ref[...], (own_count, asked_ref.shape[1]), 0)
    total[...] = near_ref[...] + dot(place, back_ref[...])
    edge = edge_ref[0]
    for j in range(n_edge // 2):
        mask = ring_mask(j)
        owner = edge ^ (2 * mask)
        for out, who in ((kept_out, owner), (sent_out, owner ^ 1)):
            out[j] = total[pl.ds(pl.multiple_of(who * rows, 8), rows), :]


def add_kernel(kept_ref, got_ref, kept_out, sent_out):
    half = kept_out.shape[0]
    kept_out[...] = kept_ref[:half] + got_ref[:half].astype(F32)
    sent_out[...] = (kept_ref[half:] + got_ref[half:].astype(F32)).astype(BF)


def last_kernel(kept_ref, got_ref, out_ref):
    out_ref[...] = kept_ref[0] + got_ref[0].astype(F32)


def paired(values):
    high = values.astype(BF).astype(F32)
    return jnp.concatenate([high, values - high], axis=0).astype(BF)


def widen(packed, rows):
    values = packed.astype(F32)
    return jnp.concatenate([values[:rows], values[rows : rows + 8] + values[rows + 8 :]], axis=0)


def chip_kernel(rows, kept_ref, got_ref, own_out, *packs):
    own_out[...] = kept_ref[0] + widen(got_ref[0], rows)
    for j, out in enumerate(packs):
        total = kept_ref[j + 1] + widen(got_ref[j + 1], rows)
        out[:rows] = total[:rows].astype(BF)
        out[rows:] = paired(total[rows:])


def total_kernel(parts, n_second, *refs):
    own_ref, gots, out_ref = refs[0], refs[1:-2], refs[-1]
    share = own_ref.shape[1] // parts
    rows = own_ref.shape[0] - 8
    lanes = out_ref.shape[1]
    total = own_ref[...]
    for ref in gots:
        total = total + widen(ref[...], rows)
    hidden = total.shape[1]
    turned = jnp.concatenate([total[:rows], jnp.zeros((lanes - rows, hidden), F32)], axis=0).T
    third = total[rows : rows + 1, :n_second]
    loss = total[rows + 1 : rows + 2, :1]
    mine = lax.broadcasted_iota(I32, (hidden, n_second), 0) % share
    mine = mine == lax.broadcasted_iota(I32, (hidden, n_second), 1) % share
    lane = lax.broadcasted_iota(I32, (n_second, lanes), 1) - rows
    group = lax.broadcasted_iota(I32, (n_second, lanes), 0) // share
    groups = n_second // share
    for part, values in enumerate(halves(third)):
        spread = jnp.where(mine, jnp.broadcast_to(values.astype(F32), (hidden, n_second)), 0.0)
        turned = turned + dot(
            spread.astype(BF), jnp.where(lane == group + part * groups, 1.0, 0.0).astype(BF)
        )
    lane = lax.broadcasted_iota(I32, (hidden, lanes), 1) - rows - 2 * groups
    for part, values in enumerate(halves(loss)):
        turned = turned + jnp.where(lane == part, values.astype(F32), 0.0)
    out_ref[...] = turned.astype(BF)


def final_kernel(rows1, rows2, got_ref, first_out, second_out, third_out, loss_out):
    total = jnp.sum(got_ref[...].astype(F32), axis=0)
    share, lanes = total.shape
    rows = rows1 + rows2
    n_second = third_out.shape[1]
    groups = n_second // share
    first_out[...] = total[:, :rows1]
    second_out[...] = total[:, rows1:rows]
    lane = lax.broadcasted_iota(I32, (lanes, n_second), 0) - rows
    group = lax.broadcasted_iota(I32, (lanes, n_second), 1) // share
    take = jnp.where((lane == group) | (lane == group + groups), 1.0, 0.0)
    spread = lax.dot_general(
        total, take, (((1,), (0,)), ((), ())),
        precision=lax.Precision.HIGHEST, preferred_element_type=F32,
    )
    mine = lax.broadcasted_iota(I32, (share, n_second), 0)
    mine = mine == lax.broadcasted_iota(I32, (share, n_second), 1) % share
    third_out[...] = jnp.sum(jnp.where(mine, spread, 0.0), axis=0, keepdims=True)
    place = rows + 2 * groups
    loss_out[...] = total[0:1, place : place + 1] + total[0:1, place + 1 : place + 2]


def body(node_rows, w_first, w_second, w_third, src_row, requests, slot_index, labels, live_count):
    own_count, width = node_rows.shape
    edges = src_row.shape[0]
    parts, cap = requests.shape
    n_edge = lax.axis_size("edge")
    chips = n_edge // 2
    slots = parts * cap
    hidden, hidden2 = w_second.shape
    scale = 1.0 / math.sqrt(edges * parts * n_edge)
    edge = lax.axis_index("edge").astype(I32).reshape(1)
    sibling = [(i, i ^ 1) for i in range(n_edge)]

    def ahead(step):
        return [(i, (i + 2 * step) % n_edge) for i in range(n_edge)]

    steps = tuple(range(2, chips - 1)) + (1, chips - 1)
    rows1 = 3 * width // n_edge
    rows2 = hidden2 // n_edge
    rows = rows1 + rows2
    cols = jnp.stack([src_row, slot_index, labels], axis=1)
    lines = jnp.stack([src_row, slot_index], axis=0)

    asked_here = lax.all_to_all(requests, "dom", split_axis=0, concat_axis=0, tiled=True)
    answer, asked_line = pl.pallas_call(
        answer_kernel,
        out_shape=(
            pltpu.HBM((slots, width), BF),
            jax.ShapeDtypeStruct((1, slots), I32),
        ),
        in_specs=[WHOLE, FAR],
        out_specs=(FAR, WHOLE),
        scratch_shapes=[
            pltpu.VMEM((own_count, width), BF),
            pltpu.VMEM((slots, width), BF),
            pltpu.SemaphoreType.DMA((3,)),
        ],
        compiler_params=params(8),
        name="answer",
    )(asked_here, in_hbm(node_rows))
    replies = lax.all_to_all(
        answer.reshape(parts, cap, width), "dom", split_axis=0, concat_axis=0, tiled=True
    ).reshape(slots, width)

    outs = [(slots, width), (edges, hidden), (chips, rows + 8, hidden), (chips, rows + 16, hidden)]
    slot_grad, back_first, kept, sent = pl.pallas_call(
        functools.partial(pair_kernel, scale, n_edge),
        out_shape=tuple(pltpu.HBM(shape, dtype) for shape, dtype in zip(outs, (BF, BF, F32, BF))),
        in_specs=[SCALARS] * 2 + [WHOLE] * 4 + [FAR] + [WHOLE] * 2,
        out_specs=(FAR,) * 4,
        scratch_shapes=[
            pltpu.VMEM((3 * width, hidden), BF),
            pltpu.VMEM((slots, width), BF),
            pltpu.VMEM((edges, hidden), BF),
            pltpu.VMEM((edges, hidden), BF),
            pltpu.VMEM((edges, hidden2), BF),
            pltpu.VMEM((3 * width, hidden), F32),
            pltpu.VMEM((hidden2, hidden), F32),
            pltpu.VMEM((8, hidden), F32),
            pltpu.VMEM((chips, rows + 16, hidden), BF),
            pltpu.VMEM((3, edges, width), BF),
            pltpu.SemaphoreType.DMA((3,)),
            pltpu.SemaphoreType.DMA((edges // TILE + 1 + 4 * chips,)),
        ],
        compiler_params=params(48),
        cost_estimate=cost(6 * 10**9, 8 * MIB),
        name="pair",
    )(live_count, edge, cols, lines, node_rows, replies, in_hbm(w_first), w_second, w_third.reshape(1, hidden2))

    returned = lax.all_to_all(
        slot_grad.reshape(parts, cap, width), "dom", split_axis=0, concat_axis=0, tiled=True
    ).reshape(slots, width)

    near_part = pl.pallas_call(
        near_kernel,
        out_shape=jax.ShapeDtypeStruct((own_count, width), F32),
        in_specs=[WHOLE] * 5,
        out_specs=WHOLE,
        compiler_params=params(32),
        cost_estimate=FREE,
        name="near",
    )(lines, cols, replies, back_first, w_first)

    pack = jax.ShapeDtypeStruct((rows + 16, hidden), BF)
    own, *packs = pl.pallas_call(
        functools.partial(chip_kernel, rows),
        out_shape=(jax.ShapeDtypeStruct((rows + 8, hidden), F32),) + (pack,) * (chips - 1),
        in_specs=[WHOLE] * 2,
        out_specs=(WHOLE,) * chips,
        compiler_params=params(16),
        cost_estimate=FREE,
        name="chip",
    )(kept, lax.ppermute(sent, "edge", sibling))
    gots = [lax.ppermute(packs[step - 1], "edge", ahead(step)) for step in steps]

    share = hidden // parts
    lanes = -(-(rows + 2 * (hidden2 // share) + 2) // 128) * 128
    packed = pl.pallas_call(
        functools.partial(total_kernel, parts, hidden2),
        out_shape=jax.ShapeDtypeStruct((hidden, lanes), BF),
        in_specs=[WHOLE] * chips + [ANYWHERE],
        out_specs=WHOLE,
        compiler_params=params(16),
        cost_estimate=FREE,
        name="total",
    )(own, *gots, near_part)
    block = jax.ShapeDtypeStruct((chips, own_count // n_edge, width), F32)
    kept, sent, packed = pl.pallas_call(
        functools.partial(owned_kernel, n_edge),
        out_shape=(block, block, jax.ShapeDtypeStruct(packed.shape, BF)),
        in_specs=[SCALARS] + [WHOLE] * 3 + [ANYWHERE],
        out_specs=(WHOLE, WHOLE, ANYWHERE),
        input_output_aliases={4: 2},
        scratch_shapes=[pltpu.VMEM((own_count, width), F32)],
        compiler_params=params(8),
        cost_estimate=FREE,
        name="owned",
    )(edge, asked_line, near_part, returned, packed)
    got = lax.all_to_all(
        packed.reshape(parts, share, lanes), "dom", split_axis=0, concat_axis=0, tiled=True
    )
    first_t, second_share, third_total, loss_total = pl.pallas_call(
        functools.partial(final_kernel, rows1, rows2),
        out_shape=(
            jax.ShapeDtypeStruct((share, rows1), F32),
            jax.ShapeDtypeStruct((share, rows2), F32),
            jax.ShapeDtypeStruct((1, hidden2), F32),
            jax.ShapeDtypeStruct((1, 1), F32),
        ),
        in_specs=[WHOLE],
        out_specs=(WHOLE,) * 4,
        compiler_params=params(8),
        cost_estimate=FREE,
        name="final",
    )(got)

    for mask in (0, 1, 3):
        partner = sibling if mask == 0 else [(i, i ^ (2 * mask)) for i in range(n_edge)]
        got = lax.ppermute(sent, "edge", partner)
        if mask == 3:
            break
        half = (kept.shape[0] // 2,) + kept.shape[1:]
        kept, sent = pl.pallas_call(
            add_kernel,
            out_shape=(jax.ShapeDtypeStruct(half, F32), jax.ShapeDtypeStruct(half, BF)),
            in_specs=[WHOLE] * 2,
            out_specs=(WHOLE,) * 2,
            compiler_params=params(8),
            cost_estimate=FREE,
            name="add",
        )(kept, got)
    node_share = pl.pallas_call(
        last_kernel,
        out_shape=jax.ShapeDtypeStruct(kept.shape[1:], F32),
        in_specs=[WHOLE] * 2,
        out_specs=WHOLE,
        compiler_params=params(8),
        cost_estimate=cost(LAST, 0),
        name="last",
    )(kept, got)
    return (
        first_t.T, second_share, third_total.reshape(hidden2), loss_total.reshape(()), node_share
    )


def solution(mesh):
    in_specs = (
        P("dom", None),
        P(),
        P(),
        P(),
        P(("dom", "edge")),
        P(("dom", "edge"), None),
        P(("dom", "edge")),
        P(("dom", "edge")),
        P(("dom", "edge")),
    )
    out_specs = (P("edge", "dom"), P("dom", "edge"), P(), P(), P(("dom", "edge"), None))
    return jax.shard_map(body, mesh=mesh, in_specs=in_specs, out_specs=out_specs, check_vma=False)
```

```python
import functools
import math

import jax
import jax.numpy as jnp
from jax import lax
from jax.experimental import pallas as pl
from jax.experimental.pallas import tpu as pltpu
from jax.sharding import PartitionSpec as P

BF = jnp.bfloat16
F32 = jnp.float32
I32 = jnp.int32
MIB = 1 << 20
TILE = 1024
LAST = 0
WHOLE = pl.BlockSpec(memory_space=pltpu.VMEM)
FREE = pl.CostEstimate(flops=0, bytes_accessed=0, transcendentals=0)
ANYWHERE = pl.BlockSpec(memory_space=pl.ANY)
FAR = pl.BlockSpec(memory_space=pltpu.HBM)
SCALARS = pl.BlockSpec(memory_space=pltpu.SMEM)


def dot(left, right, left_dim=1, right_dim=0):
    return lax.dot_general(
        left, right, (((left_dim,), (right_dim,)), ((), ())), preferred_element_type=F32
    )


def halves(values):
    high = values.astype(BF)
    return high, (values - high.astype(F32)).astype(BF)


def ring_mask(j):
    return (0, 3, 1, 2)[j]


def onehot(index, shape, axis):
    return jnp.where(index == lax.broadcasted_iota(I32, shape, axis), 1.0, 0.0).astype(BF)


def params(mib):
    return pltpu.CompilerParams(vmem_limit_bytes=mib * MIB)


def in_hbm(array):
    return pltpu.with_memory_space_constraint(array, pltpu.HBM)


def cost(flops, nbytes):
    return pl.CostEstimate(flops=flops, bytes_accessed=nbytes, transcendentals=0)


def answer_kernel(asked_ref, node_any, out_any, line_out, node_ref, out_ref, sems):
    fetch = pltpu.make_async_copy(node_any, node_ref, sems.at[0])
    fetch.start()
    parts, cap = asked_ref.shape
    own_count, slots = node_ref.shape[0], line_out.shape[1]
    spread = lax.broadcasted_iota(I32, (parts, slots), 0)
    spread = spread == lax.broadcasted_iota(I32, (parts, slots), 1) // cap
    lines = dot(asked_ref[...].astype(F32).astype(BF), jnp.where(spread, 1.0, 0.0).astype(BF), 0, 0)
    mine = lax.broadcasted_iota(I32, (cap, slots), 0)
    mine = mine == lax.broadcasted_iota(I32, (cap, slots), 1) % cap
    line = jnp.sum(jnp.where(mine, lines, 0.0), axis=0, keepdims=True).astype(I32)
    line_out[...] = line
    pick = onehot(line, (own_count, slots), 0)
    fetch.wait()
    half = slots // 2
    stores = []
    for h in range(2):
        part = pl.ds(h * half, half)
        out_ref[part] = dot(pick[:, h * half : (h + 1) * half], node_ref[...], 0, 0).astype(BF)
        stores.append(pltpu.make_async_copy(out_ref.at[part], out_any.at[part], sems.at[1 + h]))
        stores[-1].start()
    for copy in stores:
        copy.wait()


def pair_kernel(
    n_edge, live_ref, edge_ref, cols_ref, lines_ref, node_ref, rep_ref, wf_any, ws_ref, wt_ref,
    slot_out, bfirst_out, kept_out, sent_out,
    wf_ref, slot_ref, first_ref, bfirst_ref, bsecond_ref, grads, grads2, extra_ref, sent_ref,
    feat_ref, fetch_sems, store_sems,
):
    edges = cols_ref.shape[0]
    own_count, width = node_ref.shape
    slots = rep_ref.shape[0]
    hidden2 = ws_ref.shape[1]
    fetch = []
    for i in range(3):
        part = pl.ds(i * width, width)
        fetch.append(pltpu.make_async_copy(wf_any.at[part], wf_ref.at[part], fetch_sems.at[i]))
        fetch[-1].start()
    stores = []

    def store(src, dst):
        copy = pltpu.make_async_copy(src, dst, store_sems.at[len(stores)])
        copy.start()
        stores.append(copy)

    w_third = wt_ref[...].astype(F32)
    third = None
    loss = None
    for tile in range(edges // TILE):
        part = pl.ds(tile * TILE, TILE)
        near = dot(onehot(cols_ref[part, 0:1], (TILE, own_count), 1), node_ref[...])
        far = dot(onehot(cols_ref[part, 1:2], (TILE, slots), 1), rep_ref[...])
        target = cols_ref[part, 2:3].astype(F32)
        blocks = (near.astype(BF), far.astype(BF), (near * far).astype(BF))
        pre_first = None
        for i, block in enumerate(blocks):
            feat_ref[i, part] = block
            if tile == 0:
                fetch[i].wait()
            term = dot(block, wf_ref[i * width : (i + 1) * width])
            pre_first = term if pre_first is None else pre_first + term
        sig = jax.nn.sigmoid(pre_first)
        first = (pre_first * sig).astype(BF)
        slope_first = sig * (1.0 + pre_first * (1.0 - sig))
        first_ref[part] = first
        pre_second = dot(first, ws_ref[...])
        sig = jax.nn.sigmoid(pre_second)
        second_b = (pre_second * sig).astype(BF)
        second = second_b.astype(F32)
        slope_second = sig * (1.0 + pre_second * (1.0 - sig))
        logits = dot(second_b, jnp.broadcast_to(wt_ref[...], (hidden2, hidden2)), 1, 1)
        place = tile * TILE + lax.broadcasted_iota(I32, (TILE, hidden2), 0)
        live = jnp.where(place < live_ref[0], 1.0, 0.0)
        slope = live * (jax.nn.sigmoid(logits) - target)
        back_second = (slope * w_third * slope_second).astype(BF)
        bsecond_ref[part] = back_second
        back_first = (dot(back_second, ws_ref[...], 1, 1) * slope_first).astype(BF)
        bfirst_ref[part] = back_first
        store(bfirst_ref.at[part], bfirst_out.at[part])
        softplus = jnp.maximum(logits, 0.0) + jnp.log1p(jnp.exp(-jnp.abs(logits)))
        term = jnp.sum(live * (softplus - target * logits), axis=0, keepdims=True)
        loss = term if loss is None else loss + term
        term = jnp.sum(slope * second, axis=0, keepdims=True)
        third = term if third is None else third + term
    extra_ref[...] = jnp.zeros_like(extra_ref)
    extra_ref[0:1, :hidden2] = third
    extra_ref[1:2, :hidden2] = loss

    rows1 = 3 * width // n_edge
    rows2 = hidden2 // n_edge
    rows = rows1 + rows2
    bfirst = bfirst_ref[...]
    grads2[...] = dot(bsecond_ref[...], first_ref[...], 0, 0)
    for i in range(3):
        grads[i * width : (i + 1) * width] = dot(feat_ref[i], bfirst, 0, 0)
    edge = edge_ref[0]
    chip = edge // 2
    core = edge % 2
    chips = n_edge // 2
    extra = paired(extra_ref[...])
    for j in range(chips):
        there = 2 * ((chip + j) % chips)
        part1 = pl.ds(pl.multiple_of((there + core) * rows1, 8), rows1)
        part2 = pl.ds(pl.multiple_of((there + core) * rows2, 8), rows2)
        store(grads.at[part1], kept_out.at[j, pl.ds(0, rows1)])
        store(grads2.at[part2], kept_out.at[j, pl.ds(rows1, rows2)])
        store(extra_ref, kept_out.at[j, pl.ds(rows, 8)])
        part1 = pl.ds(pl.multiple_of((there + 1 - core) * rows1, 8), rows1)
        part2 = pl.ds(pl.multiple_of((there + 1 - core) * rows2, 8), rows2)
        sent_ref[j, :rows1] = grads[part1, :].astype(BF)
        sent_ref[j, rows1:rows] = grads2[part2, :].astype(BF)
        sent_ref[j, rows:] = extra
        store(sent_ref.at[j], sent_out.at[j])

    total = None
    for tile in range(edges // TILE):
        part = pl.ds(tile * TILE, TILE)
        back_first = bfirst_ref[part]
        block_b = dot(back_first, wf_ref[width : 2 * width], 1, 1)
        block_c = dot(back_first, wf_ref[2 * width :], 1, 1)
        place = onehot(lines_ref[1:2, part], (slots, TILE), 0)
        term = dot(place, (block_b + block_c * feat_ref[0, part].astype(F32)).astype(BF))
        total = term if total is None else total + term
    slot_ref[...] = total.astype(BF)
    store(slot_ref, slot_out)
    for copy in stores:
        copy.wait()


def near_kernel(lines_ref, cols_ref, rep_ref, bfirst_ref, wf_ref, out_ref):
    edges = lines_ref.shape[1]
    slots, width = rep_ref.shape
    bfirst = bfirst_ref[...]
    far = dot(onehot(cols_ref[:, 1:2], (edges, slots), 1), rep_ref[...])
    block_a = dot(bfirst, wf_ref[:width], 1, 1)
    block_c = dot(bfirst, wf_ref[2 * width :], 1, 1)
    high, low = halves(block_a + block_c * far)
    place = onehot(lines_ref[0:1, :], (out_ref.shape[0], edges), 0)
    out_ref[...] = dot(place, high) + dot(place, low)


def owned_kernel(n_edge, edge_ref, asked_ref, near_ref, back_ref, packed_ref, kept_out, sent_out, packed_out, total):
    own_count = near_ref.shape[0]
    rows = own_count // n_edge
    place = onehot(asked_ref[...], (own_count, asked_ref.shape[1]), 0)
    total[...] = near_ref[...] + dot(place, back_ref[...])
    edge = edge_ref[0]
    for j in range(n_edge // 2):
        owner = edge ^ (2 * ring_mask(j))
        kept_out[j] = total[pl.ds(pl.multiple_of(owner * rows, 8), rows), :]
        part = pl.ds(pl.multiple_of((owner ^ 1) * rows, 8), rows)
        sent_out[j] = total[part, :].astype(BF)


def add_kernel(kept_ref, got_ref, kept_out, sent_out):
    half = kept_out.shape[0]
    kept_out[...] = kept_ref[:half] + got_ref[:half].astype(F32)
    sent_out[...] = (kept_ref[half:] + got_ref[half:].astype(F32)).astype(BF)


def last_kernel(kept_ref, got_ref, out_ref):
    out_ref[...] = kept_ref[0] + got_ref[0].astype(F32)


def paired(values):
    high = values.astype(BF).astype(F32)
    return jnp.concatenate([high, values - high], axis=0).astype(BF)


def widen(packed, rows):
    values = packed.astype(F32)
    return jnp.concatenate([values[:rows], values[rows : rows + 8] + values[rows + 8 :]], axis=0)


def chip_kernel(rows, kept_ref, got_ref, own_out, *packs):
    own_out[...] = kept_ref[0] + widen(got_ref[0], rows)
    for j, out in enumerate(packs):
        total = kept_ref[j + 1] + widen(got_ref[j + 1], rows)
        out[:rows] = total[:rows].astype(BF)
        out[rows:] = paired(total[rows:])


def total_kernel(parts, n_second, *refs):
    own_ref, gots, out_ref = refs[0], refs[1:-2], refs[-1]
    share = own_ref.shape[1] // parts
    rows = own_ref.shape[0] - 8
    lanes = out_ref.shape[1]
    total = own_ref[...]
    for ref in gots:
        total = total + widen(ref[...], rows)
    hidden = total.shape[1]
    turned = jnp.concatenate([total[:rows], jnp.zeros((lanes - rows, hidden), F32)], axis=0).T
    third = total[rows : rows + 1, :n_second]
    loss = total[rows + 1 : rows + 2, :1]
    mine = lax.broadcasted_iota(I32, (hidden, n_second), 0) % share
    mine = mine == lax.broadcasted_iota(I32, (hidden, n_second), 1) % share
    lane = lax.broadcasted_iota(I32, (n_second, lanes), 1) - rows
    group = lax.broadcasted_iota(I32, (n_second, lanes), 0) // share
    groups = n_second // share
    for part, values in enumerate(halves(third)):
        spread = jnp.where(mine, jnp.broadcast_to(values.astype(F32), (hidden, n_second)), 0.0)
        turned = turned + dot(
            spread.astype(BF), jnp.where(lane == group + part * groups, 1.0, 0.0).astype(BF)
        )
    lane = lax.broadcasted_iota(I32, (hidden, lanes), 1) - rows - 2 * groups
    for part, values in enumerate(halves(loss)):
        turned = turned + jnp.where(lane == part, values.astype(F32), 0.0)
    out_ref[...] = turned.astype(BF)


def final_kernel(scale, rows1, rows2, got_ref, first_out, second_out, third_out, loss_out):
    total = scale * jnp.sum(got_ref[...].astype(F32), axis=0)
    share, lanes = total.shape
    rows = rows1 + rows2
    n_second = third_out.shape[1]
    groups = n_second // share
    first_out[...] = total[:, :rows1]
    second_out[...] = total[:, rows1:rows]
    lane = lax.broadcasted_iota(I32, (lanes, n_second), 0) - rows
    group = lax.broadcasted_iota(I32, (lanes, n_second), 1) // share
    take = jnp.where((lane == group) | (lane == group + groups), 1.0, 0.0)
    spread = lax.dot_general(
        total, take, (((1,), (0,)), ((), ())),
        precision=lax.Precision.HIGHEST, preferred_element_type=F32,
    )
    mine = lax.broadcasted_iota(I32, (share, n_second), 0)
    mine = mine == lax.broadcasted_iota(I32, (share, n_second), 1) % share
    third_out[...] = jnp.sum(jnp.where(mine, spread, 0.0), axis=0, keepdims=True)
    place = rows + 2 * groups
    loss_out[...] = total[0:1, place : place + 1] + total[0:1, place + 1 : place + 2]


def body(node_rows, w_first, w_second, w_third, src_row, requests, slot_index, labels, live_count):
    own_count, width = node_rows.shape
    edges = src_row.shape[0]
    parts, cap = requests.shape
    n_edge = lax.axis_size("edge")
    chips = n_edge // 2
    slots = parts * cap
    hidden, hidden2 = w_second.shape
    scale = 1.0 / math.sqrt(edges * parts * n_edge)
    edge = lax.axis_index("edge").astype(I32).reshape(1)
    sibling = [(i, i ^ 1) for i in range(n_edge)]

    def ahead(step):
        return [(i, (i + 2 * step) % n_edge) for i in range(n_edge)]

    steps = tuple(range(2, chips - 1)) + (1, chips - 1)
    rows1 = 3 * width // n_edge
    rows2 = hidden2 // n_edge
    rows = rows1 + rows2
    cols = jnp.stack([src_row, slot_index, labels], axis=1)
    lines = jnp.stack([src_row, slot_index], axis=0)

    asked_here = lax.all_to_all(requests, "dom", split_axis=0, concat_axis=0, tiled=True)
    answer, asked_line = pl.pallas_call(
        answer_kernel,
        out_shape=(
            pltpu.HBM((slots, width), BF),
            jax.ShapeDtypeStruct((1, slots), I32),
        ),
        in_specs=[WHOLE, FAR],
        out_specs=(FAR, WHOLE),
        scratch_shapes=[
            pltpu.VMEM((own_count, width), BF),
            pltpu.VMEM((slots, width), BF),
            pltpu.SemaphoreType.DMA((3,)),
        ],
        compiler_params=params(8),
        name="answer",
    )(asked_here, in_hbm(node_rows))
    replies = lax.all_to_all(
        answer.reshape(parts, cap, width), "dom", split_axis=0, concat_axis=0, tiled=True
    ).reshape(slots, width)

    outs = [(slots, width), (edges, hidden), (chips, rows + 8, hidden), (chips, rows + 16, hidden)]
    slot_grad, back_first, kept, sent = pl.pallas_call(
        functools.partial(pair_kernel, n_edge),
        out_shape=tuple(pltpu.HBM(shape, dtype) for shape, dtype in zip(outs, (BF, BF, F32, BF))),
        in_specs=[SCALARS] * 2 + [WHOLE] * 4 + [FAR] + [WHOLE] * 2,
        out_specs=(FAR,) * 4,
        scratch_shapes=[
            pltpu.VMEM((3 * width, hidden), BF),
            pltpu.VMEM((slots, width), BF),
            pltpu.VMEM((edges, hidden), BF),
            pltpu.VMEM((edges, hidden), BF),
            pltpu.VMEM((edges, hidden2), BF),
            pltpu.VMEM((3 * width, hidden), F32),
            pltpu.VMEM((hidden2, hidden), F32),
            pltpu.VMEM((8, hidden), F32),
            pltpu.VMEM((chips, rows + 16, hidden), BF),
            pltpu.VMEM((3, edges, width), BF),
            pltpu.SemaphoreType.DMA((3,)),
            pltpu.SemaphoreType.DMA((edges // TILE + 1 + 4 * chips,)),
        ],
        compiler_params=params(48),
        cost_estimate=cost(6 * 10**9, 8 * MIB),
        name="pair",
    )(live_count, edge, cols, lines, node_rows, replies, in_hbm(w_first), w_second, w_third.reshape(1, hidden2))

    returned = lax.all_to_all(
        slot_grad.reshape(parts, cap, width), "dom", split_axis=0, concat_axis=0, tiled=True
    ).reshape(slots, width)

    near_part = pl.pallas_call(
        near_kernel,
        out_shape=jax.ShapeDtypeStruct((own_count, width), F32),
        in_specs=[WHOLE] * 5,
        out_specs=WHOLE,
        compiler_params=params(32),
        cost_estimate=FREE,
        name="near",
    )(lines, cols, replies, back_first, w_first)

    pack = jax.ShapeDtypeStruct((rows + 16, hidden), BF)
    own, *packs = pl.pallas_call(
        functools.partial(chip_kernel, rows),
        out_shape=(jax.ShapeDtypeStruct((rows + 8, hidden), F32),) + (pack,) * (chips - 1),
        in_specs=[WHOLE] * 2,
        out_specs=(WHOLE,) * chips,
        compiler_params=params(16),
        cost_estimate=FREE,
        name="chip",
    )(kept, lax.ppermute(sent, "edge", sibling))
    gots = [lax.ppermute(packs[step - 1], "edge", ahead(step)) for step in steps]

    share = hidden // parts
    lanes = -(-(rows + 2 * (hidden2 // share) + 2) // 128) * 128
    packed = pl.pallas_call(
        functools.partial(total_kernel, parts, hidden2),
        out_shape=jax.ShapeDtypeStruct((hidden, lanes), BF),
        in_specs=[WHOLE] * chips + [ANYWHERE],
        out_specs=WHOLE,
        compiler_params=params(16),
        cost_estimate=FREE,
        name="total",
    )(own, *gots, near_part)
    block = jax.ShapeDtypeStruct((chips, own_count // n_edge, width), F32)
    kept, sent, packed = pl.pallas_call(
        functools.partial(owned_kernel, n_edge),
        out_shape=(
            block,
            jax.ShapeDtypeStruct(block.shape, BF),
            jax.ShapeDtypeStruct(packed.shape, BF),
        ),
        in_specs=[SCALARS] + [WHOLE] * 3 + [ANYWHERE],
        out_specs=(WHOLE, WHOLE, ANYWHERE),
        input_output_aliases={4: 2},
        scratch_shapes=[pltpu.VMEM((own_count, width), F32)],
        compiler_params=params(8),
        cost_estimate=FREE,
        name="owned",
    )(edge, asked_line, near_part, returned, packed)
    got = lax.all_to_all(
        packed.reshape(parts, share, lanes), "dom", split_axis=0, concat_axis=0, tiled=True
    )
    first_t, second_share, third_total, loss_total = pl.pallas_call(
        functools.partial(final_kernel, scale, rows1, rows2),
        out_shape=(
            jax.ShapeDtypeStruct((share, rows1), F32),
            jax.ShapeDtypeStruct((share, rows2), F32),
            jax.ShapeDtypeStruct((1, hidden2), F32),
            jax.ShapeDtypeStruct((1, 1), F32),
        ),
        in_specs=[WHOLE],
        out_specs=(WHOLE,) * 4,
        compiler_params=params(8),
        cost_estimate=FREE,
        name="final",
    )(got)

    for mask in (0, 1, 3):
        partner = sibling if mask == 0 else [(i, i ^ (2 * mask)) for i in range(n_edge)]
        got = lax.ppermute(sent, "edge", partner)
        if mask == 3:
            break
        half = (kept.shape[0] // 2,) + kept.shape[1:]
        kept, sent = pl.pallas_call(
            add_kernel,
            out_shape=(jax.ShapeDtypeStruct(half, F32), jax.ShapeDtypeStruct(half, BF)),
            in_specs=[WHOLE] * 2,
            out_specs=(WHOLE,) * 2,
            compiler_params=params(8),
            cost_estimate=FREE,
            name="add",
        )(kept, got)
    node_share = pl.pallas_call(
        last_kernel,
        out_shape=jax.ShapeDtypeStruct(kept.shape[1:], F32),
        in_specs=[WHOLE] * 2,
        out_specs=WHOLE,
        compiler_params=params(8),
        cost_estimate=cost(LAST, 0),
        name="last",
    )(kept, got)
    return (
        first_t.T, second_share, third_total.reshape(hidden2), loss_total.reshape(()), node_share
    )


def solution(mesh):
    in_specs = (
        P("dom", None),
        P(),
        P(),
        P(),
        P(("dom", "edge")),
        P(("dom", "edge"), None),
        P(("dom", "edge")),
        P(("dom", "edge")),
        P(("dom", "edge")),
    )
    out_specs = (P("edge", "dom"), P("dom", "edge"), P(), P(), P(("dom", "edge"), None))
    return jax.shard_map(body, mesh=mesh, in_specs=in_specs, out_specs=out_specs, check_vma=False)
```

```python
import functools
import math

import jax
import jax.numpy as jnp
from jax import lax
from jax.experimental import pallas as pl
from jax.experimental.pallas import tpu as pltpu
from jax.sharding import PartitionSpec as P

BF = jnp.bfloat16
F32 = jnp.float32
I32 = jnp.int32
MIB = 1 << 20
TILE = 512
LAST = 0
WHOLE = pl.BlockSpec(memory_space=pltpu.VMEM)
FREE = pl.CostEstimate(flops=0, bytes_accessed=0, transcendentals=0)
ANYWHERE = pl.BlockSpec(memory_space=pl.ANY)
FAR = pl.BlockSpec(memory_space=pltpu.HBM)
SCALARS = pl.BlockSpec(memory_space=pltpu.SMEM)


def dot(left, right, left_dim=1, right_dim=0):
    return lax.dot_general(
        left, right, (((left_dim,), (right_dim,)), ((), ())), preferred_element_type=F32
    )


def halves(values):
    high = values.astype(BF)
    return high, (values - high.astype(F32)).astype(BF)


def ring_mask(j):
    return (0, 3, 1, 2)[j]


def onehot(index, shape, axis):
    return jnp.where(index == lax.broadcasted_iota(I32, shape, axis), 1.0, 0.0).astype(BF)


def params(mib):
    return pltpu.CompilerParams(vmem_limit_bytes=mib * MIB)


def in_hbm(array):
    return pltpu.with_memory_space_constraint(array, pltpu.HBM)


def cost(flops, nbytes):
    return pl.CostEstimate(flops=flops, bytes_accessed=nbytes, transcendentals=0)


def answer_kernel(asked_ref, node_any, out_any, line_out, node_ref, out_ref, sems):
    fetch = pltpu.make_async_copy(node_any, node_ref, sems.at[0])
    fetch.start()
    parts, cap = asked_ref.shape
    own_count, slots = node_ref.shape[0], line_out.shape[1]
    spread = lax.broadcasted_iota(I32, (parts, slots), 0)
    spread = spread == lax.broadcasted_iota(I32, (parts, slots), 1) // cap
    lines = dot(asked_ref[...].astype(F32).astype(BF), jnp.where(spread, 1.0, 0.0).astype(BF), 0, 0)
    mine = lax.broadcasted_iota(I32, (cap, slots), 0)
    mine = mine == lax.broadcasted_iota(I32, (cap, slots), 1) % cap
    line = jnp.sum(jnp.where(mine, lines, 0.0), axis=0, keepdims=True).astype(I32)
    line_out[...] = line
    pick = onehot(line, (own_count, slots), 0)
    fetch.wait()
    half = slots // 2
    stores = []
    for h in range(2):
        part = pl.ds(h * half, half)
        out_ref[part] = dot(pick[:, h * half : (h + 1) * half], node_ref[...], 0, 0).astype(BF)
        stores.append(pltpu.make_async_copy(out_ref.at[part], out_any.at[part], sems.at[1 + h]))
        stores[-1].start()
    for copy in stores:
        copy.wait()


def pair_kernel(
    scale, n_edge, live_ref, edge_ref, cols_ref, lines_ref, node_ref, rep_ref, wf_any, ws_ref, wt_ref,
    slot_out, bfirst_out, kept_out, sent_out,
    wf_ref, slot_ref, first_ref, bfirst_ref, bsecond_ref, grads, grads2, extra_ref, sent_ref,
    feat_ref, fetch_sems, store_sems,
):
    edges = cols_ref.shape[0]
    own_count, width = node_ref.shape
    slots = rep_ref.shape[0]
    hidden2 = ws_ref.shape[1]
    fetch = []
    for i in range(3):
        part = pl.ds(i * width, width)
        fetch.append(pltpu.make_async_copy(wf_any.at[part], wf_ref.at[part], fetch_sems.at[i]))
        fetch[-1].start()
    stores = []

    def store(src, dst):
        copy = pltpu.make_async_copy(src, dst, store_sems.at[len(stores)])
        copy.start()
        stores.append(copy)

    w_third = wt_ref[...].astype(F32)
    third = None
    loss = None
    for tile in range(edges // TILE):
        part = pl.ds(tile * TILE, TILE)
        near = dot(onehot(cols_ref[part, 0:1], (TILE, own_count), 1), node_ref[...])
        far = dot(onehot(cols_ref[part, 1:2], (TILE, slots), 1), rep_ref[...])
        target = cols_ref[part, 2:3].astype(F32)
        blocks = (near.astype(BF), far.astype(BF), (near * far).astype(BF))
        pre_first = None
        for i, block in enumerate(blocks):
            feat_ref[i, part] = block
            if tile == 0:
                fetch[i].wait()
            term = dot(block, wf_ref[i * width : (i + 1) * width])
            pre_first = term if pre_first is None else pre_first + term
        sig = jax.nn.sigmoid(pre_first)
        first = (pre_first * sig).astype(BF)
        slope_first = sig * (1.0 + pre_first * (1.0 - sig))
        first_ref[part] = first
        pre_second = dot(first, ws_ref[...])
        sig = jax.nn.sigmoid(pre_second)
        second_b = (pre_second * sig).astype(BF)
        second = second_b.astype(F32)
        slope_second = sig * (1.0 + pre_second * (1.0 - sig))
        logits = dot(second_b, jnp.broadcast_to(wt_ref[...], (hidden2, hidden2)), 1, 1)
        place = tile * TILE + lax.broadcasted_iota(I32, (TILE, hidden2), 0)
        live = jnp.where(place < live_ref[0], 1.0, 0.0)
        slope = live * (jax.nn.sigmoid(logits) - target)
        back_second = (slope * w_third * slope_second).astype(BF)
        bsecond_ref[part] = back_second
        back_first = (dot(back_second, ws_ref[...], 1, 1) * slope_first).astype(BF)
        bfirst_ref[part] = back_first
        store(bfirst_ref.at[part], bfirst_out.at[part])
        softplus = jnp.maximum(logits, 0.0) + jnp.log1p(jnp.exp(-jnp.abs(logits)))
        term = jnp.sum(live * (softplus - target * logits), axis=0, keepdims=True)
        loss = term if loss is None else loss + term
        term = jnp.sum(slope * second, axis=0, keepdims=True)
        third = term if third is None else third + term
    extra_ref[...] = jnp.zeros_like(extra_ref)
    extra_ref[0:1, :hidden2] = scale * third
    extra_ref[1:2, :hidden2] = scale * loss

    rows1 = 3 * width // n_edge
    rows2 = hidden2 // n_edge
    rows = rows1 + rows2
    bfirst = bfirst_ref[...]
    grads2[...] = scale * dot(bsecond_ref[...], first_ref[...], 0, 0)
    for i in range(3):
        grads[i * width : (i + 1) * width] = scale * dot(feat_ref[i], bfirst, 0, 0)
    edge = edge_ref[0]
    chip = edge // 2
    core = edge % 2
    chips = n_edge // 2
    extra = paired(extra_ref[...])
    for j in range(chips):
        there = 2 * ((chip + j) % chips)
        part1 = pl.ds(pl.multiple_of((there + core) * rows1, 8), rows1)
        part2 = pl.ds(pl.multiple_of((there + core) * rows2, 8), rows2)
        store(grads.at[part1], kept_out.at[j, pl.ds(0, rows1)])
        store(grads2.at[part2], kept_out.at[j, pl.ds(rows1, rows2)])
        store(extra_ref, kept_out.at[j, pl.ds(rows, 8)])
        part1 = pl.ds(pl.multiple_of((there + 1 - core) * rows1, 8), rows1)
        part2 = pl.ds(pl.multiple_of((there + 1 - core) * rows2, 8), rows2)
        sent_ref[j, :rows1] = grads[part1, :].astype(BF)
        sent_ref[j, rows1:rows] = grads2[part2, :].astype(BF)
        sent_ref[j, rows:] = extra
        store(sent_ref.at[j], sent_out.at[j])

    total = None
    for tile in range(edges // TILE):
        part = pl.ds(tile * TILE, TILE)
        back_first = bfirst_ref[part]
        block_b = dot(back_first, wf_ref[width : 2 * width], 1, 1)
        block_c = dot(back_first, wf_ref[2 * width :], 1, 1)
        place = onehot(lines_ref[1:2, part], (slots, TILE), 0)
        term = dot(place, (block_b + block_c * feat_ref[0, part].astype(F32)).astype(BF))
        total = term if total is None else total + term
    slot_ref[...] = total.astype(BF)
    store(slot_ref, slot_out)
    for copy in stores:
        copy.wait()


def near_kernel(lines_ref, cols_ref, rep_ref, bfirst_ref, wf_ref, out_ref):
    edges = lines_ref.shape[1]
    slots, width = rep_ref.shape
    bfirst = bfirst_ref[...]
    far = dot(onehot(cols_ref[:, 1:2], (edges, slots), 1), rep_ref[...])
    block_a = dot(bfirst, wf_ref[:width], 1, 1)
    block_c = dot(bfirst, wf_ref[2 * width :], 1, 1)
    high, low = halves(block_a + block_c * far)
    place = onehot(lines_ref[0:1, :], (out_ref.shape[0], edges), 0)
    out_ref[...] = dot(place, high) + dot(place, low)


def owned_kernel(n_edge, edge_ref, asked_ref, near_ref, back_ref, packed_ref, kept_out, sent_out, packed_out, total):
    own_count = near_ref.shape[0]
    rows = own_count // n_edge
    place = onehot(asked_ref[...], (own_count, asked_ref.shape[1]), 0)
    total[...] = near_ref[...] + dot(place, back_ref[...])
    edge = edge_ref[0]
    for j in range(n_edge // 2):
        mask = ring_mask(j)
        owner = edge ^ (2 * mask)
        for out, who in ((kept_out, owner), (sent_out, owner ^ 1)):
            out[j] = total[pl.ds(pl.multiple_of(who * rows, 8), rows), :]


def add_kernel(kept_ref, got_ref, kept_out, sent_out):
    half = kept_out.shape[0]
    kept_out[...] = kept_ref[:half] + got_ref[:half].astype(F32)
    sent_out[...] = (kept_ref[half:] + got_ref[half:].astype(F32)).astype(BF)


def last_kernel(kept_ref, got_ref, out_ref):
    out_ref[...] = kept_ref[0] + got_ref[0].astype(F32)


def paired(values):
    high = values.astype(BF).astype(F32)
    return jnp.concatenate([high, values - high], axis=0).astype(BF)


def widen(packed, rows):
    values = packed.astype(F32)
    return jnp.concatenate([values[:rows], values[rows : rows + 8] + values[rows + 8 :]], axis=0)


def chip_kernel(rows, kept_ref, got_ref, own_out, *packs):
    own_out[...] = kept_ref[0] + widen(got_ref[0], rows)
    for j, out in enumerate(packs):
        total = kept_ref[j + 1] + widen(got_ref[j + 1], rows)
        out[:rows] = total[:rows].astype(BF)
        out[rows:] = paired(total[rows:])


def total_kernel(parts, n_second, *refs):
    own_ref, gots, out_ref = refs[0], refs[1:-2], refs[-1]
    share = own_ref.shape[1] // parts
    rows = own_ref.shape[0] - 8
    lanes = out_ref.shape[1]
    total = own_ref[...]
    for ref in gots:
        total = total + widen(ref[...], rows)
    hidden = total.shape[1]
    turned = jnp.concatenate([total[:rows], jnp.zeros((lanes - rows, hidden), F32)], axis=0).T
    third = total[rows : rows + 1, :n_second]
    loss = total[rows + 1 : rows + 2, :1]
    mine = lax.broadcasted_iota(I32, (hidden, n_second), 0) % share
    mine = mine == lax.broadcasted_iota(I32, (hidden, n_second), 1) % share
    lane = lax.broadcasted_iota(I32, (n_second, lanes), 1) - rows
    group = lax.broadcasted_iota(I32, (n_second, lanes), 0) // share
    groups = n_second // share
    for part, values in enumerate(halves(third)):
        spread = jnp.where(mine, jnp.broadcast_to(values.astype(F32), (hidden, n_second)), 0.0)
        turned = turned + dot(
            spread.astype(BF), jnp.where(lane == group + part * groups, 1.0, 0.0).astype(BF)
        )
    lane = lax.broadcasted_iota(I32, (hidden, lanes), 1) - rows - 2 * groups
    for part, values in enumerate(halves(loss)):
        turned = turned + jnp.where(lane == part, values.astype(F32), 0.0)
    out_ref[...] = turned.astype(BF)


def final_kernel(rows1, rows2, got_ref, first_out, second_out, third_out, loss_out):
    total = jnp.sum(got_ref[...].astype(F32), axis=0)
    share, lanes = total.shape
    rows = rows1 + rows2
    n_second = third_out.shape[1]
    groups = n_second // share
    first_out[...] = total[:, :rows1]
    second_out[...] = total[:, rows1:rows]
    lane = lax.broadcasted_iota(I32, (lanes, n_second), 0) - rows
    group = lax.broadcasted_iota(I32, (lanes, n_second), 1) // share
    take = jnp.where((lane == group) | (lane == group + groups), 1.0, 0.0)
    spread = lax.dot_general(
        total, take, (((1,), (0,)), ((), ())),
        precision=lax.Precision.HIGHEST, preferred_element_type=F32,
    )
    mine = lax.broadcasted_iota(I32, (share, n_second), 0)
    mine = mine == lax.broadcasted_iota(I32, (share, n_second), 1) % share
    third_out[...] = jnp.sum(jnp.where(mine, spread, 0.0), axis=0, keepdims=True)
    place = rows + 2 * groups
    loss_out[...] = total[0:1, place : place + 1] + total[0:1, place + 1 : place + 2]


def body(node_rows, w_first, w_second, w_third, src_row, requests, slot_index, labels, live_count):
    own_count, width = node_rows.shape
    edges = src_row.shape[0]
    parts, cap = requests.shape
    n_edge = lax.axis_size("edge")
    chips = n_edge // 2
    slots = parts * cap
    hidden, hidden2 = w_second.shape
    scale = 1.0 / math.sqrt(edges * parts * n_edge)
    edge = lax.axis_index("edge").astype(I32).reshape(1)
    sibling = [(i, i ^ 1) for i in range(n_edge)]

    def ahead(step):
        return [(i, (i + 2 * step) % n_edge) for i in range(n_edge)]

    steps = tuple(range(2, chips - 1)) + (1, chips - 1)
    rows1 = 3 * width // n_edge
    rows2 = hidden2 // n_edge
    rows = rows1 + rows2
    cols = jnp.stack([src_row, slot_index, labels], axis=1)
    lines = jnp.stack([src_row, slot_index], axis=0)

    asked_here = lax.all_to_all(requests, "dom", split_axis=0, concat_axis=0, tiled=True)
    answer, asked_line = pl.pallas_call(
        answer_kernel,
        out_shape=(
            pltpu.HBM((slots, width), BF),
            jax.ShapeDtypeStruct((1, slots), I32),
        ),
        in_specs=[WHOLE, FAR],
        out_specs=(FAR, WHOLE),
        scratch_shapes=[
            pltpu.VMEM((own_count, width), BF),
            pltpu.VMEM((slots, width), BF),
            pltpu.SemaphoreType.DMA((3,)),
        ],
        compiler_params=params(8),
        name="answer",
    )(asked_here, in_hbm(node_rows))
    replies = lax.all_to_all(
        answer.reshape(parts, cap, width), "dom", split_axis=0, concat_axis=0, tiled=True
    ).reshape(slots, width)

    outs = [(slots, width), (edges, hidden), (chips, rows + 8, hidden), (chips, rows + 16, hidden)]
    slot_grad, back_first, kept, sent = pl.pallas_call(
        functools.partial(pair_kernel, scale, n_edge),
        out_shape=tuple(pltpu.HBM(shape, dtype) for shape, dtype in zip(outs, (BF, BF, F32, BF))),
        in_specs=[SCALARS] * 2 + [WHOLE] * 4 + [FAR] + [WHOLE] * 2,
        out_specs=(FAR,) * 4,
        scratch_shapes=[
            pltpu.VMEM((3 * width, hidden), BF),
            pltpu.VMEM((slots, width), BF),
            pltpu.VMEM((edges, hidden), BF),
            pltpu.VMEM((edges, hidden), BF),
            pltpu.VMEM((edges, hidden2), BF),
            pltpu.VMEM((3 * width, hidden), F32),
            pltpu.VMEM((hidden2, hidden), F32),
            pltpu.VMEM((8, hidden), F32),
            pltpu.VMEM((chips, rows + 16, hidden), BF),
            pltpu.VMEM((3, edges, width), BF),
            pltpu.SemaphoreType.DMA((3,)),
            pltpu.SemaphoreType.DMA((edges // TILE + 1 + 4 * chips,)),
        ],
        compiler_params=params(48),
        cost_estimate=cost(6 * 10**9, 8 * MIB),
        name="pair",
    )(live_count, edge, cols, lines, node_rows, replies, in_hbm(w_first), w_second, w_third.reshape(1, hidden2))

    returned = lax.all_to_all(
        slot_grad.reshape(parts, cap, width), "dom", split_axis=0, concat_axis=0, tiled=True
    ).reshape(slots, width)

    near_part = pl.pallas_call(
        near_kernel,
        out_shape=jax.ShapeDtypeStruct((own_count, width), F32),
        in_specs=[WHOLE] * 5,
        out_specs=WHOLE,
        compiler_params=params(32),
        cost_estimate=FREE,
        name="near",
    )(lines, cols, replies, back_first, w_first)

    pack = jax.ShapeDtypeStruct((rows + 16, hidden), BF)
    own, *packs = pl.pallas_call(
        functools.partial(chip_kernel, rows),
        out_shape=(jax.ShapeDtypeStruct((rows + 8, hidden), F32),) + (pack,) * (chips - 1),
        in_specs=[WHOLE] * 2,
        out_specs=(WHOLE,) * chips,
        compiler_params=params(16),
        cost_estimate=FREE,
        name="chip",
    )(kept, lax.ppermute(sent, "edge", sibling))
    gots = [lax.ppermute(packs[step - 1], "edge", ahead(step)) for step in steps]

    share = hidden // parts
    lanes = -(-(rows + 2 * (hidden2 // share) + 2) // 128) * 128
    packed = pl.pallas_call(
        functools.partial(total_kernel, parts, hidden2),
        out_shape=jax.ShapeDtypeStruct((hidden, lanes), BF),
        in_specs=[WHOLE] * chips + [ANYWHERE],
        out_specs=WHOLE,
        compiler_params=params(16),
        cost_estimate=FREE,
        name="total",
    )(own, *gots, near_part)
    block = jax.ShapeDtypeStruct((chips, own_count // n_edge, width), F32)
    kept, sent, packed = pl.pallas_call(
        functools.partial(owned_kernel, n_edge),
        out_shape=(block, block, jax.ShapeDtypeStruct(packed.shape, BF)),
        in_specs=[SCALARS] + [WHOLE] * 3 + [ANYWHERE],
        out_specs=(WHOLE, WHOLE, ANYWHERE),
        input_output_aliases={4: 2},
        scratch_shapes=[pltpu.VMEM((own_count, width), F32)],
        compiler_params=params(8),
        cost_estimate=FREE,
        name="owned",
    )(edge, asked_line, near_part, returned, packed)
    got = lax.all_to_all(
        packed.reshape(parts, share, lanes), "dom", split_axis=0, concat_axis=0, tiled=True
    )
    first_t, second_share, third_total, loss_total = pl.pallas_call(
        functools.partial(final_kernel, rows1, rows2),
        out_shape=(
            jax.ShapeDtypeStruct((share, rows1), F32),
            jax.ShapeDtypeStruct((share, rows2), F32),
            jax.ShapeDtypeStruct((1, hidden2), F32),
            jax.ShapeDtypeStruct((1, 1), F32),
        ),
        in_specs=[WHOLE],
        out_specs=(WHOLE,) * 4,
        compiler_params=params(8),
        cost_estimate=FREE,
        name="final",
    )(got)

    for mask in (0, 1, 3):
        partner = sibling if mask == 0 else [(i, i ^ (2 * mask)) for i in range(n_edge)]
        got = lax.ppermute(sent, "edge", partner)
        if mask == 3:
            break
        half = (kept.shape[0] // 2,) + kept.shape[1:]
        kept, sent = pl.pallas_call(
            add_kernel,
            out_shape=(jax.ShapeDtypeStruct(half, F32), jax.ShapeDtypeStruct(half, BF)),
            in_specs=[WHOLE] * 2,
            out_specs=(WHOLE,) * 2,
            compiler_params=params(8),
            cost_estimate=FREE,
            name="add",
        )(kept, got)
    node_share = pl.pallas_call(
        last_kernel,
        out_shape=jax.ShapeDtypeStruct(kept.shape[1:], F32),
        in_specs=[WHOLE] * 2,
        out_specs=WHOLE,
        compiler_params=params(8),
        cost_estimate=cost(LAST, 0),
        name="last",
    )(kept, got)
    return (
        first_t.T, second_share, third_total.reshape(hidden2), loss_total.reshape(()), node_share
    )


def solution(mesh):
    in_specs = (
        P("dom", None),
        P(),
        P(),
        P(),
        P(("dom", "edge")),
        P(("dom", "edge"), None),
        P(("dom", "edge")),
        P(("dom", "edge")),
        P(("dom", "edge")),
    )
    out_specs = (P("edge", "dom"), P("dom", "edge"), P(), P(), P(("dom", "edge"), None))
    return jax.shard_map(body, mesh=mesh, in_specs=in_specs, out_specs=out_specs, check_vma=False)
```
